32 devices in a mesh: dp: 8 (over z, y), expert: 4 (over x, core).
Axes of the slice: x: 2, y: 2, z: 4, core: 2. Of those that a mesh axis runs over, the one named last changes fastest.
Arguments:
- residual_input: bfloat16 [8192, 1024], P(('dp', 'expert')), may hold values from -6 to 6
- prompt_token_length: int32 [48], replicated, may hold values from 1 to 1024, 8192 in all
- prompt_adapter_index: int32 [48], replicated, may hold values from 0 to 63
- adapter_table_row: int32 [64], replicated, may hold values from 0 to 63, each once
- adapter_norm_gain: bfloat16 [1024], replicated, may hold values from 0.5 to 1.5
- adapter_down_maps: bfloat16 [64, 16, 1024], P('expert'), may hold values from -0.1875 to 0.1875
- adapter_up_maps: bfloat16 [64, 16, 1024], P('expert'), may hold values from -1.5 to 1.5
- expert_norm_gain: bfloat16 [1024], replicated, may hold values from 0.5 to 1.5
- router: bfloat16 [1024, 4], replicated, may hold values from -0.1875 to 0.1875
- token_expert_index: int32 [8192, 2], P(('dp', 'expert')), may hold values from 0 to 3, all different within a row; in each aligned block of 256 rows (0 to 255, 256 to 511, ...) at most 160 rows name the same one
- expert_gate_up_weight: bfloat16 [4, 2, 1024, 2816], P('expert', None, None, 'dp'), may hold values from -0.1875 to 0.1875
- expert_down_weight: bfloat16 [4, 2816, 1024], P('expert', None, 'dp'), may hold values from -0.109375 to 0.109375
Outputs:
- layer_out: bfloat16 [8192, 1024], P(('dp', 'expert'))
The draws below stay inside these ranges and needn't reach their ends.
Inputs may be any that keep to these rules, and one draw needn't show every extreme that they name: `prompt_token_length`: the lengths sum to 8192; the longest is exactly 1024. `adapter_table_row`: each adapter has its own row of adapter_down_maps and adapter_up_maps: a permutation. `token_expert_index`: the two ids of a token differ. Within the 256 rows of one device no expert is named by more than 160 rows, a bound that some block reaches.
All inputs are finite; a program needn't handle non-finite values.
Results may differ from the reference program's by a relative error of at most 0.0064.
Values may be sent and summed in bfloat16 or wider, within the bound.
No kernel may reach another device: no remote copies, remote signals or barrier semaphores. Data moves between devices by JAX's collectives and lax.ppermute only.
A program may use at most 128 MiB of HBM per device.

```python
import math
import jax
import jax.numpy as jnp
import numpy as np
from jax import lax

MODEL_WIDTH = 1024
FF = 2816
ADAPTER_RANK = 16
ADAPTER_COUNT = 64
TOP = 2
TOK_DEV = 256
EXPERTS = 4
CAP = 160
TOKENS = 8192
PROMPTS = 48
LONGEST = 1024


def with_ends(drawn, stream_key, low, high):
    spot = [jax.random.randint(jax.random.fold_in(stream_key, axis), (), 0, length) for axis, length in enumerate(drawn.shape)]
    widest = drawn.shape.index(max(drawn.shape))
    beside = spot[:widest] + [(spot[widest] + 1) % drawn.shape[widest]] + spot[widest + 1:]
    return drawn.at[tuple(spot)].set(low).at[tuple(beside)].set(high)


def block_levels(rng, shape, split, least, high):
    def one(dim, parts):
        draws = jax.random.uniform(jax.random.fold_in(jax.random.fold_in(rng, 6), dim), (parts,), jnp.float32, least / len(split), high / len(split))
        return jnp.repeat(jnp.exp(draws), shape[dim] // parts).reshape((-1,) + (1,) * (len(shape) - dim - 1))

    factor_of = one(*split[0])
    for cut in split[1:]:
        factor_of = factor_of * one(*cut)
    return factor_of


def rank_table(count, skew):
    portions = [(1 << 20) // math.isqrt(standing ** skew) + 1 for standing in range(1, count + 1)]
    spread = 1 + sum(portions) // (1 << 30)
    return np.cumsum(np.array([max(1, weight // spread) for weight in portions]))


def ranked_ids(rng, dims, amount, slope):
    table = rank_table(amount, slope)
    lot = jax.random.randint(jax.random.fold_in(rng, 1), dims, 0, int(table[amount - 1]))
    grade = jnp.searchsorted(jnp.asarray(table, jnp.int32), lot, side="right")
    return jax.random.permutation(jax.random.fold_in(rng, 2), amount)[grade].astype(jnp.int32)


def profile(count, total, reach, slope):
    portions = [(1 << 20) // math.isqrt(rank ** slope) + 1 for rank in range(2, count + 1)]
    rest, holding = total - reach - (count - 1), [1] * (count - 1)
    while rest > 0:
        free = [i for i in range(count - 1) if holding[i] < reach]
        mass, remaining = sum([portions[i] for i in free]), rest
        for i in free:
            addition = min(reach - holding[i], max(1, remaining * portions[i] // mass), rest)
            holding[i] = holding[i] + addition
            rest = rest - addition
    return np.array([reach] + holding)


def ragged_sizes(own_key, count, total, bound, lean):
    if count == 2:
        one = jax.random.randint(own_key, (), max(1, total - bound), min(bound, total - 1) + 1)
        return jnp.stack([one, total - one])
    sizes = jnp.asarray(profile(count, total, bound, lean), jnp.int32)
    couples = (count - 1) // 2
    source_of, taker = sizes[1:1 + 2 * couples:2], sizes[2:2 + 2 * couples:2]
    room = jnp.minimum(source_of - 1, bound - taker)
    shifted = jax.random.randint(jax.random.fold_in(own_key, 1), (couples,), 0, 1 << 20) % (room + 1)
    sizes = sizes.at[1:1 + 2 * couples:2].set(source_of - shifted).at[2:2 + 2 * couples:2].set(taker + shifted)
    return sizes[jax.random.permutation(jax.random.fold_in(own_key, 2), count)]


def deal_out(stream_key, own, number, rows, number_of, top, limit, slope):
    ranking = jax.random.permutation(stream_key, number_of)
    packed, ordinary = load_shares(number_of, rows * top, limit, slope, True), load_shares(number_of, rows * top, limit, slope, False)
    places = jnp.arange(number_of)

    def named(sizes, offset_by):
        used = int((sizes > 0).sum())
        fixed = max(1, used // 4)
        moved = fixed + (places - fixed + offset_by * (used - fixed)) % max(1, number_of - fixed)
        return jnp.zeros((number_of,), jnp.int32).at[ranking[jnp.where(places < fixed, places, moved)]].set(jnp.asarray(sizes, jnp.int32))

    sizes = jnp.where(number % 4 == 0, named(packed, number // 4), named(ordinary, number - number // 4 - 1))
    mixed = jax.random.permutation(jax.random.fold_in(own, 3), number_of)
    source_of, receiver = mixed[0:number_of // 2 * 2:2], mixed[1:number_of // 2 * 2:2]
    margin = jnp.minimum(sizes[source_of] - 1, limit - sizes[receiver]) // 2
    margin = jnp.where((source_of == ranking[0]) | (receiver == ranking[0]) | (sizes[receiver] == 0), 0, jnp.maximum(margin, 0))
    moved = jax.random.randint(jax.random.fold_in(own, 4), (number_of // 2,), 0, 1 << 20) % (margin + 1)
    sizes = sizes.at[source_of].add(-moved).at[receiver].add(moved)
    items = jnp.searchsorted(jnp.cumsum(sizes), jnp.arange(rows * top), side="right").astype(jnp.int32)
    grid = items.reshape(top, rows).T
    grid = grid[jax.random.permutation(jax.random.fold_in(own, 1), rows)]
    offset_by = jax.random.randint(jax.random.fold_in(own, 2), (rows, 1), 0, top)
    return jnp.take_along_axis(grid, (jnp.arange(top)[None, :] + offset_by) % top, axis=1)


def load_shares(count, total, limit, skew, full):
    loads = [(1 << 20) // math.isqrt(rank ** skew) + 1 for rank in range(1, count + 1)]
    largest = limit if full else min(limit, max(-(-total // count), total * loads[0] // sum(loads)))
    least = 1 if total - largest >= count - 1 else 0
    counts, rest = [largest] + [least] * (count - 1), total - largest - least * (count - 1)
    while rest > 0:
        movable = [i for i in range(1, count) if counts[i] < largest] or [i for i in range(1, count) if counts[i] < limit]
        mass, left = sum([loads[i] for i in movable]), rest
        for i in movable:
            extra = min(limit - counts[i], max(1, left * loads[i] // mass), rest)
            counts[i] = counts[i] + extra
            rest = rest - extra
    return np.array(counts)


def bell_draw(stream_key, shape, spread, most, shards=(), kind=jnp.bfloat16):
    drawn = jax.random.normal(stream_key, shape, jnp.float32) * spread
    if len(shards) > 0:
        drawn = block_levels(stream_key, shape, shards, -0.22, 0.18) * drawn
    return jnp.clip(drawn, min=-most, max=most).astype(kind)


def setup_inputs(seed: int = 0) -> dict:
    arg_keys = jax.random.split(jax.random.key(seed), 13)
    residual_input = bell_draw(arg_keys[0], (TOKENS, MODEL_WIDTH), 1.0, 6.0, ((0, 32),))
    prompt_token_length = ragged_sizes(arg_keys[1], PROMPTS, TOKENS, LONGEST, 2).astype(jnp.int32)
    prompt_adapter_index = with_ends(ranked_ids(arg_keys[2], (PROMPTS,), ADAPTER_COUNT, 1), jax.random.fold_in(arg_keys[2], 3), 0, ADAPTER_COUNT - 1).astype(jnp.int32)
    adapter_table_row = jax.random.permutation(arg_keys[3], ADAPTER_COUNT).astype(jnp.int32)
    adapter_norm_gain = jnp.clip(1.0 + 0.1 * jax.random.normal(arg_keys[4], (MODEL_WIDTH,), jnp.float32), 0.5, 1.5).astype(jnp.bfloat16)
    adapter_down_maps = bell_draw(arg_keys[5], (ADAPTER_COUNT, ADAPTER_RANK, MODEL_WIDTH), MODEL_WIDTH ** -0.5, 0.1875, ((0, 4),))
    adapter_up_maps = bell_draw(arg_keys[6], (ADAPTER_COUNT, ADAPTER_RANK, MODEL_WIDTH), ADAPTER_RANK ** -0.5, 1.5, ((0, 4),))
    expert_norm_gain = jnp.clip(1.0 + 0.1 * jax.random.normal(arg_keys[7], (MODEL_WIDTH,), jnp.float32), 0.5, 1.5).astype(jnp.bfloat16)
    router = bell_draw(arg_keys[8], (MODEL_WIDTH, EXPERTS), MODEL_WIDTH ** -0.5, 0.1875)
    token_expert_index_keys = jax.random.split(jax.random.fold_in(arg_keys[9], 1), TOKENS // TOK_DEV)
    token_expert_index_turns = jax.random.permutation(jax.random.fold_in(arg_keys[9], 3), TOKENS // TOK_DEV)
    token_expert_index = jax.vmap(lambda own, number: deal_out(jax.random.fold_in(arg_keys[9], 2), own, number, TOK_DEV, EXPERTS, TOP, CAP, 2))(token_expert_index_keys, token_expert_index_turns).reshape((TOKENS, TOP))
    expert_gate_up_weight = bell_draw(arg_keys[10], (EXPERTS, 2, MODEL_WIDTH, FF), MODEL_WIDTH ** -0.5, 0.1875, ((0, 4), (3, 8)))
    expert_down_weight = bell_draw(arg_keys[11], (EXPERTS, FF, MODEL_WIDTH), FF ** -0.5, 0.109375, ((0, 4), (2, 8)))
    return dict(residual_input=residual_input, prompt_token_length=prompt_token_length, prompt_adapter_index=prompt_adapter_index, adapter_table_row=adapter_table_row, adapter_norm_gain=adapter_norm_gain, adapter_down_maps=adapter_down_maps, adapter_up_maps=adapter_up_maps, expert_norm_gain=expert_norm_gain, router=router, token_expert_index=token_expert_index, expert_gate_up_weight=expert_gate_up_weight, expert_down_weight=expert_down_weight)


def rms_norm(values, gain):
    stat = lax.optimization_barrier(jnp.mean(values * values, axis=-1, keepdims=True))
    return values * lax.rsqrt(stat + 1e-06) * gain.astype(jnp.float32)

def reference(residual_input, prompt_token_length, prompt_adapter_index, adapter_table_row, adapter_norm_gain, adapter_down_maps, adapter_up_maps, expert_norm_gain, router, token_expert_index, expert_gate_up_weight, expert_down_weight):
    blocks = TOKENS // TOK_DEV
    ends = jnp.cumsum(prompt_token_length).astype(jnp.int32)
    starts = (ends - prompt_token_length).astype(jnp.int32)
    down_adapter_table = adapter_down_maps.reshape(ADAPTER_COUNT * ADAPTER_RANK, MODEL_WIDTH)
    up_adapter_table = adapter_up_maps.reshape(ADAPTER_COUNT * ADAPTER_RANK, MODEL_WIDTH)
    column_slot = (jnp.arange(ADAPTER_COUNT * ADAPTER_RANK, dtype=jnp.int32) // ADAPTER_RANK).astype(jnp.int32)
    adapter_ids = jnp.arange(ADAPTER_COUNT, dtype=jnp.int32)
    expert_range = jnp.arange(EXPERTS, dtype=jnp.int32)

    def front(inputs):
        block, states, ids = inputs
        positions = (block * TOK_DEV + jnp.arange(TOK_DEV, dtype=jnp.int32)).astype(jnp.int32)
        inside = (positions[:, None] >= starts[None, :]) & (positions[:, None] < ends[None, :])
        adapter = lax.optimization_barrier(jnp.sum(jnp.where(inside, prompt_adapter_index[None, :], 0), axis=1)).astype(jnp.int32)
        slot = lax.optimization_barrier(jnp.sum(jnp.where(adapter[:, None] == adapter_ids[None, :], adapter_table_row[None, :], 0), axis=1)).astype(jnp.int32)
        floats = states.astype(jnp.float32)
        normed = rms_norm(floats, adapter_norm_gain).astype(jnp.bfloat16)
        low_all = lax.dot_general(normed, down_adapter_table, (((1,), (1,)), ((), ())), preferred_element_type=jnp.float32)
        low = jnp.where(column_slot[None, :] == slot[:, None], low_all, 0.0).astype(jnp.bfloat16)
        delta = jnp.dot(low, up_adapter_table, preferred_element_type=jnp.float32)
        mixed = (floats + 2.0 * delta).astype(jnp.bfloat16)
        expert_in = rms_norm(mixed.astype(jnp.float32), expert_norm_gain).astype(jnp.bfloat16)
        logits = jnp.dot(expert_in, router, preferred_element_type=jnp.float32)
        prob = jax.nn.sigmoid(jnp.take_along_axis(logits, ids, axis=1))
        onehot = (ids.reshape(-1)[:, None] == expert_range[None, :]).astype(jnp.int32)
        running = (jnp.cumsum(onehot, axis=0) - 1).astype(jnp.int32)
        pos = lax.optimization_barrier(jnp.sum(onehot * running, axis=1)).astype(jnp.int32).reshape(TOK_DEV, TOP)
        return (mixed, expert_in, prob, pos)
    block_ids = jnp.arange(blocks, dtype=jnp.int32)
    mixed, expert_in, prob, pos = lax.map(front, (block_ids, residual_input.reshape(blocks, TOK_DEV, MODEL_WIDTH), token_expert_index.reshape(blocks, TOK_DEV, TOP)))
    ids = token_expert_index.reshape(blocks, TOK_DEV, TOP)
    rows = (block_ids[:, None, None] * CAP + pos).astype(jnp.int32)
    values = jnp.broadcast_to(expert_in[:, :, None, :], (blocks, TOK_DEV, TOP, MODEL_WIDTH))
    buffer = jnp.zeros((EXPERTS, blocks * CAP, MODEL_WIDTH), jnp.bfloat16).at[ids, rows].set(values)

    def expert_ffn(inputs):
        rows_in, gate_up, down = inputs
        gate = jnp.dot(rows_in, gate_up[0], preferred_element_type=jnp.float32)
        up = jnp.dot(rows_in, gate_up[1], preferred_element_type=jnp.float32)
        act = (jax.nn.gelu(gate, approximate=True) * up).astype(jnp.bfloat16)
        return jnp.dot(act, down, preferred_element_type=jnp.float32).astype(jnp.bfloat16)
    outputs = lax.map(expert_ffn, (buffer, expert_gate_up_weight, expert_down_weight))
    picked = outputs[ids, rows].astype(jnp.float32)
    total = mixed.astype(jnp.float32) + lax.optimization_barrier(jnp.sum(prob[..., None] * picked, axis=2))
    return total.astype(jnp.bfloat16).reshape(TOKENS, MODEL_WIDTH)
```

```python
import jax
import jax.numpy as jnp
from jax import lax
from jax.sharding import Mesh
from jax.sharding import PartitionSpec as P

CORES = 2


def rms_norm(values, gain):
    stat = jnp.mean(values * values, axis=-1, keepdims=True)
    return values * lax.rsqrt(stat + 1e-06) * gain.astype(jnp.float32)


def dot(a, b):
    return jnp.dot(a, b, preferred_element_type=jnp.float32)


def from_offset(value, axis, size, offset):
    if offset % size == 0:
        return value
    return lax.ppermute(value, axis, [((i + offset) % size, i) for i in range(size)])


def on_device(
    sizes,
    residual_input,
    prompt_token_length,
    prompt_adapter_index,
    adapter_table_row,
    adapter_norm_gain,
    adapter_down_maps,
    adapter_up_maps,
    expert_norm_gain,
    router,
    token_expert_index,
    expert_gate_up_weight,
    expert_down_weight,
):
    lines, los, exs = sizes["line"], sizes["lo"], sizes["ex"]
    tok_rows, width = residual_input.shape
    num_experts = router.shape[1]
    line, lo, ex, core = (lax.axis_index(n) for n in ("line", "lo", "ex", "core"))

    tokens = [from_offset(residual_input, "line", lines, k) for k in range(lines)]
    named = [from_offset(token_expert_index, "line", lines, k) for k in range(lines)]

    slots, rank, _ = adapter_down_maps.shape
    tables = jnp.stack([adapter_down_maps.reshape(slots * rank, width), adapter_up_maps.reshape(slots * rank, width)])
    parts, owners = [], []
    for i in range(exs):
        mine = from_offset(tables, "ex", exs, i)
        for j in range(CORES):
            parts.append(from_offset(mine, "core", CORES, j))
            owners.append((ex + i) % exs * CORES + (core + j) % CORES)
    column_slot = jnp.concatenate(
        [own * slots + jnp.arange(slots * rank, dtype=jnp.int32) // rank for own in owners]
    )
    tables_down = jnp.concatenate([p[0] for p in parts])
    tables_up = jnp.concatenate([p[1] for p in parts])

    down_rows = expert_down_weight.shape[1]
    cols = expert_down_weight.shape[2]
    down_own = lax.all_to_all(
        expert_down_weight.reshape(lines, down_rows // lines, cols), "line", split_axis=0, concat_axis=0, tiled=True
    )
    gate_up, down = [], []
    for i in range(exs):
        g = from_offset(expert_gate_up_weight[0], "ex", exs, i)
        gate_up.append([from_offset(g, "lo", los, j) for j in range(los)])
        d = from_offset(down_own, "ex", exs, i)
        down.append([from_offset(d, "lo", los, j) for j in range(los)])

    ends = jnp.cumsum(prompt_token_length)
    starts = ends - prompt_token_length
    adapter_ids = jnp.arange(adapter_table_row.shape[0], dtype=jnp.int32)
    mixed_own, expert_in, weight = None, [], []
    for k in range(lines):
        block = (((line + k) % lines * los + lo) * exs + ex) * CORES + core
        positions = block * tok_rows + jnp.arange(tok_rows, dtype=jnp.int32)
        inside = (positions[:, None] >= starts[None, :]) & (positions[:, None] < ends[None, :])
        adapter = jnp.sum(jnp.where(inside, prompt_adapter_index[None, :], 0), axis=1)
        slot = jnp.sum(
            jnp.where(adapter[:, None] == adapter_ids[None, :], adapter_table_row[None, :], 0), axis=1
        )
        floats = tokens[k].astype(jnp.float32)
        normed = rms_norm(floats, adapter_norm_gain).astype(jnp.bfloat16)
        low_all = lax.dot_general(
            normed, tables_down, (((1,), (1,)), ((), ())), preferred_element_type=jnp.float32
        )
        low = jnp.where(column_slot[None, :] == slot[:, None], low_all, 0.0).astype(jnp.bfloat16)
        mixed = (floats + 2.0 * dot(low, tables_up)).astype(jnp.bfloat16)
        if k == 0:
            mixed_own = mixed
        inner = rms_norm(mixed.astype(jnp.float32), expert_norm_gain).astype(jnp.bfloat16)
        prob = jax.nn.sigmoid(dot(inner, router))
        chosen = jnp.any(
            named[k][:, :, None] == jnp.arange(num_experts, dtype=jnp.int32)[None, None, :], axis=1
        )
        expert_in.append(inner)
        weight.append(jnp.where(chosen, prob, 0.0))
    x_own, w_own = jnp.concatenate(expert_in), jnp.concatenate(weight)
    x_far, w_far = (from_offset(v, "core", CORES, 1) for v in (x_own, w_own))

    acts = {"own": [], "far": []}
    for i in range(exs):
        gate = jnp.concatenate([g[0] for g in gate_up[i]], axis=1)
        up = jnp.concatenate([g[1] for g in gate_up[i]], axis=1)
        expert = (ex + i) % exs * CORES + core
        for name, x, w in (("far", x_far, w_far), ("own", x_own, w_own)):
            scale = jnp.sum(
                jnp.where(jnp.arange(num_experts, dtype=jnp.int32)[None, :] == expert, w, 0.0), axis=1, keepdims=True
            )
            act = jax.nn.gelu(dot(x, gate), approximate=True) * dot(x, up) * scale
            acts[name].append(act.astype(jnp.bfloat16))
    act_own, act_far = (jnp.concatenate(acts[n], axis=1) for n in ("own", "far"))

    pieces = []
    units = down_rows // lines // los
    for j in range(los):
        rows = []
        for i in range(exs):
            piece = down[i][j].reshape(lines, los, units, cols)
            ordered = jnp.roll(piece, -lo, axis=1) if los > 1 else piece
            rows.append(ordered.transpose(1, 2, 0, 3).reshape(los * units, lines * cols))
        weights = jnp.concatenate(rows)
        far = from_offset(dot(act_far, weights).astype(jnp.bfloat16), "core", CORES, 1)
        total = (dot(act_own, weights) + far.astype(jnp.float32)).astype(jnp.bfloat16)
        total = total.reshape(lines, tok_rows, lines * cols)
        home = total[0].astype(jnp.float32)
        for k in range(1, lines):
            home = home + from_offset(total[k], "line", lines, -k).astype(jnp.float32)
        pieces.append(home.reshape(tok_rows, lines, cols))
    out = jnp.roll(jnp.stack(pieces, axis=2), lo, axis=2).reshape(tok_rows, width)
    return (mixed_own.astype(jnp.float32) + out).astype(jnp.bfloat16)


def solution(mesh):
    dp, expert = mesh.shape["dp"], mesh.shape["expert"]
    lines = 4 if dp % 4 == 0 else 1
    sizes = {"line": lines, "lo": dp // lines, "ex": expert // CORES, "core": CORES}
    inner = Mesh(mesh.devices.reshape(tuple(sizes.values())), tuple(sizes))
    rows = P(("line", "lo", "ex", "core"), None)
    slots = P(("ex", "core"), None, None)
    placed = (
        rows,
        P(),
        P(),
        P(),
        P(),
        slots,
        slots,
        P(),
        P(),
        rows,
        P(("ex", "core"), None, None, ("line", "lo")),
        P(("ex", "core"), None, ("line", "lo")),
    )

    def body(*arrays):
        return on_device(sizes, *arrays)

    return jax.shard_map(body, mesh=inner, in_specs=placed, out_specs=rows, check_vma=False)
```

```python
import functools

import jax
import jax.numpy as jnp
from jax import lax
from jax.experimental import pallas as pl
from jax.experimental.pallas import tpu as pltpu
from jax.sharding import Mesh
from jax.sharding import PartitionSpec as P

CORES = 2
LANES = 128
EXTRA = 16
VMEM = 56 * 2**20


def from_offset(value, axis, size, offset):
    if offset % size == 0:
        return value
    return lax.ppermute(value, axis, [((i + offset) % size, i) for i in range(size)])


def together(*values):
    return lax.optimization_barrier(values)


def across(value, size, mask):
    return lax.ppermute(value, "line", [(i ^ mask, i) for i in range(size)]) if mask else value


def dot(a, b, rhs_dim=0):
    return lax.dot_general(a, b, (((1,), (rhs_dim,)), ((), ())), preferred_element_type=jnp.float32)


def rms_norm(values, gain):
    stat = jnp.mean(values * values, axis=-1, keepdims=True)
    return values * lax.rsqrt(stat + 1e-06) * gain.astype(jnp.float32)


def whole(array):
    return pl.BlockSpec(array.shape, lambda *_: (0,) * len(array.shape))


def brief():
    return pl.CostEstimate(flops=1, transcendentals=0, bytes_accessed=1)


def front_kernel(pieces, blocks, rows, base_ref, prompts_ref, owner_ref, gain_a_ref, gain_e_ref, router_ref, *refs):
    table_refs, refs = refs[: 2 * pieces], refs[2 * pieces :]
    token_refs, refs = refs[:blocks], refs[blocks:]
    mixed_ref, weight_ref, inner_refs = refs[0], refs[1], refs[2:]
    for k in range(blocks):
        at = base_ref[k] + lax.broadcasted_iota(jnp.int32, (rows, 1), 0)
        inside = (at >= prompts_ref[0:1, :]) & (at < prompts_ref[1:2, :])
        slot = jnp.sum(jnp.where(inside, prompts_ref[2:3, :], 0), axis=1, keepdims=True)
        floats = token_refs[k][0:rows, :].astype(jnp.float32)
        normed = rms_norm(floats, gain_a_ref[...]).astype(jnp.bfloat16)
        delta = jnp.zeros(floats.shape, jnp.float32)
        first = 0
        for p in range(pieces):
            down_ref, up_ref = table_refs[2 * p], table_refs[2 * p + 1]
            size = down_ref.shape[0]
            low = dot(normed, down_ref[...], 1)
            low = jnp.where(owner_ref[0:1, first : first + size] == slot, low, 0.0).astype(jnp.bfloat16)
            delta = delta + dot(low, up_ref[...])
            first += size
        mixed = (floats + 2.0 * delta).astype(jnp.bfloat16)
        if k == 0:
            mixed_ref[...] = mixed
        inner = rms_norm(mixed.astype(jnp.float32), gain_e_ref[...]).astype(jnp.bfloat16)
        inner_refs[k][...] = inner
        prob = jax.nn.sigmoid(dot(router_ref[...], inner, 1))
        expert = lax.broadcasted_iota(jnp.int32, (LANES, rows), 0).astype(jnp.float32)
        ids = token_refs[k][rows : rows + EXTRA, :].astype(jnp.float32)
        chosen = (ids[0:1, 0:rows] == expert) | (ids[1:2, 0:rows] == expert)
        weight_ref[k * rows : (k + 1) * rows, :] = jnp.where(chosen, prob, 0.0).T


def front(bases, prompts, owner, gain_a, gain_e, router, tables, tokens):
    rows = tokens[0].shape[0] - EXTRA
    width = tokens[0].shape[1]
    blocks = len(tokens)
    block = jax.ShapeDtypeStruct((rows, width), jnp.bfloat16)
    outs = [block, jax.ShapeDtypeStruct((blocks * rows, LANES), jnp.float32)] + [block] * blocks
    arrays = [prompts, owner, gain_a, gain_e, router, *tables, *tokens]
    mixed, weight, *inner = pl.pallas_call(
        functools.partial(front_kernel, len(tables) // 2, blocks, rows),
        out_shape=outs,
        grid=(1,),
        in_specs=[pl.BlockSpec(memory_space=pltpu.SMEM)] + [whole(a) for a in arrays],
        out_specs=[whole(a) for a in outs],
        compiler_params=pltpu.CompilerParams(vmem_limit_bytes=VMEM),
        cost_estimate=brief(),
        name="front",
    )(bases, *arrays)
    return mixed, weight, inner


def hidden(x, weight, gate, up):
    act = jax.nn.gelu(dot(x, gate, 1), approximate=True) * dot(x, up, 1) * weight
    return act.astype(jnp.bfloat16)


def final_kernel(los, lines, count, lo_ref, mixed_ref, *refs):
    out_ref = refs[-1]
    cols = mixed_ref.shape[1] // (los * lines)
    for j in range(los):
        parts = refs[j * count : (j + 1) * count]
        total = parts[0][...].astype(jnp.float32)
        for part in parts[1:]:
            total = total + part[...].astype(jnp.float32)
        for h in range(lines):
            first = (h * los + lax.rem(lo_ref[0] + j, los)) * cols
            place = pl.ds(pl.multiple_of(first, LANES), cols)
            own = mixed_ref[:, place].astype(jnp.float32)
            out_ref[:, place] = (own + total[:, h * cols : (h + 1) * cols]).astype(jnp.bfloat16)


def final(lines, lo, mixed, parts):
    los, count = len(parts), len(parts[0])
    rows, width = mixed.shape
    if width // (los * lines) % LANES:
        sums = [sum(p.astype(jnp.float32) for p in group).reshape(rows, lines, -1) for group in parts]
        total = jnp.roll(jnp.stack(sums, axis=2), lo[0], axis=2).reshape(rows, width)
        return (mixed.astype(jnp.float32) + total).astype(jnp.bfloat16)
    flat = [p for group in parts for p in group]
    return pl.pallas_call(
        functools.partial(final_kernel, los, lines, count),
        out_shape=jax.ShapeDtypeStruct(mixed.shape, jnp.bfloat16),
        grid=(1,),
        in_specs=[pl.BlockSpec(memory_space=pltpu.SMEM)] + [whole(a) for a in (mixed, *flat)],
        out_specs=whole(mixed),
        compiler_params=pltpu.CompilerParams(vmem_limit_bytes=VMEM // 4),
        cost_estimate=brief(),
        name="final",
    )(lo, mixed, *flat)


def on_device(
    sizes,
    residual_input,
    prompt_token_length,
    prompt_adapter_index,
    adapter_table_row,
    adapter_norm_gain,
    adapter_down_maps,
    adapter_up_maps,
    expert_norm_gain,
    router,
    token_expert_index,
    expert_gate_up_weight,
    expert_down_weight,
):
    lines, los, exs = sizes["line"], sizes["lo"], sizes["ex"]
    tok_rows, width = residual_input.shape
    num_experts = router.shape[1]
    line, lo, ex, core = (lax.axis_index(n) for n in ("line", "lo", "ex", "core"))

    down_rows = expert_down_weight.shape[1]
    cols = expert_down_weight.shape[2]
    slots, rank, _ = adapter_down_maps.shape
    shares = los if slots % los == 0 else 1
    share = slots // shares
    ex_far, lo_far = range(1, exs), range(1, los)

    ids = token_expert_index.T.astype(jnp.bfloat16)
    ids = jnp.pad(ids, ((0, EXTRA - ids.shape[0]), (0, width - tok_rows)))
    block = jnp.concatenate([residual_input, ids])
    maps = [m.reshape(slots * rank, width) for m in (adapter_down_maps, adapter_up_maps)]
    first = lo * share * rank if shares > 1 else 0
    sent = lax.dynamic_slice_in_dim(jnp.stack(maps), first, share * rank, axis=1)
    crossed = [from_offset(sent, "ex", exs, i) for i in ex_far]
    gate, up = expert_gate_up_weight[0, 0].T, expert_gate_up_weight[0, 1].T
    ups = {(0, j): from_offset(up, "lo", los, j) for j in lo_far}
    tokens = [across(block, lines, m) for m in range(lines) if m < 3]
    other_maps = [from_offset(m, "core", CORES, 1) for m in maps]

    ends = jnp.cumsum(prompt_token_length)
    adapter_ids = jnp.arange(adapter_table_row.shape[0], dtype=jnp.int32)
    named = prompt_adapter_index[:, None] == adapter_ids[None, :]
    prompt_row = jnp.sum(jnp.where(named, adapter_table_row[None, :], 0), axis=1)
    prompts = jnp.stack([ends - prompt_token_length, ends, prompt_row])
    router_rows = jnp.pad(router.T, ((0, LANES - num_experts), (0, 0)))
    offsets = line ^ jnp.arange(lines, dtype=jnp.int32)
    bases = (((offsets * los + lo) * exs + ex) * CORES + core) * tok_rows
    number = jnp.arange(slots * rank, dtype=jnp.int32) // rank
    owners = [(ex * CORES + core) * slots + number]
    for i in ex_far:
        for j in range(shares):
            start = ((ex + i) % exs * CORES + core) * slots + (lo + j) % los * share
            owners.append(start + number[: share * rank])
    owner = jnp.concatenate(owners)
    owner = jnp.concatenate([owner, owner + jnp.where(core == 0, slots, -slots)])[None, :]
    small = [bases, prompts, owner, adapter_norm_gain[None], expert_norm_gain[None], router_rows]

    gate, up, small, crossed, ups, tokens = together(gate, up, small, crossed, ups, tokens)
    passed = [from_offset(c, "lo", los, j) for c in crossed for j in range(shares)]
    gates = {(i, 0): from_offset(gate, "ex", exs, i) for i in ex_far}
    if lines == 4:
        tokens = tokens + [across(tokens[2], lines, 1)]

    gate, up, down, passed, gates, tokens = together(gate, up, expert_down_weight, passed, gates, tokens)
    held = [[jnp.concatenate([p[m] for p in passed[i * shares : (i + 1) * shares]]) for m in range(2)] for i in range(exs - 1)]
    held_other = [[from_offset(m, "core", CORES, 1) for m in h] for h in held]
    gates.update({(0, j): from_offset(gate, "lo", los, j) for j in lo_far})
    ups.update({(i, 0): from_offset(up, "ex", exs, i) for i in ex_far})
    down = lax.all_to_all(
        down.reshape(lines, down_rows // lines, cols), "line", split_axis=0, concat_axis=2, tiled=True
    ).reshape(down_rows // lines, lines * cols)
    tables = [m for pair in [maps] + held + [other_maps] + held_other for m in pair]
    mixed, w_own, x_own = front(*small, tables, tokens)

    x_own, w_own, gates, ups, gate, up, down = together(x_own, w_own, gates, ups, gate, up, down)
    gates[0, 0], ups[0, 0] = gate, up
    for i in ex_far:
        for j in lo_far:
            gates[i, j] = from_offset(gates[i, 0], "lo", los, j)
            ups[i, j] = from_offset(ups[0, j], "ex", exs, i)
    x_far = [from_offset(v, "core", CORES, 1) for v in x_own]
    w_far = from_offset(w_own, "core", CORES, 1)
    column = jnp.arange(LANES, dtype=jnp.int32)[None, :]

    def act(i, x, w):
        expert = (ex + i) % exs * CORES + core
        scale = jnp.sum(jnp.where(column == expert, w, 0.0), axis=1, keepdims=True)
        gate, up = (jnp.concatenate([of[i, j] for j in range(los)]) for of in (gates, ups))
        return hidden(jnp.concatenate(x), scale, gate, up)

    near, far = [act(0, x_own, w_own)], [act(0, x_far, w_far)]

    x_own, w_own, x_far, w_far, near, far, gates, ups, down = together(
        x_own, w_own, x_far, w_far, near, far, gates, ups, down
    )
    downs = {(i, 0): from_offset(down, "ex", exs, i) for i in range(exs)}
    downs.update({(0, j): from_offset(down, "lo", los, j) for j in lo_far})
    far += [act(i, x_far, w_far) for i in ex_far]
    near += [act(i, x_own, w_own) for i in ex_far]

    def in_order(piece):
        rows = piece.reshape(los, -1, piece.shape[1])
        picked = []
        for j in range(los):
            value = rows[0]
            for a in range(1, los):
                value = jnp.where((lo + j) % los == a, rows[a], value)
            picked.append(value)
        return jnp.concatenate(picked)

    near, far, downs = together(near, far, downs)
    for i in ex_far:
        for j in lo_far:
            if exs == los == 2:
                half = down.shape[0] // 2
                upper = from_offset(downs[i, 0][:half], "lo", los, j)
                lower = from_offset(downs[0, j][half:], "ex", exs, i)
                downs[i, j] = jnp.concatenate([upper, lower])
            else:
                downs[i, j] = from_offset(downs[i, 0], "lo", los, j)
    parts = []
    for j in range(los):
        pieces = [in_order(downs[i, j]) for i in range(exs)]
        project = lambda acts: sum(dot(a, d) for a, d in zip(acts, pieces))
        sent = project(far).astype(jnp.bfloat16).reshape(lines, tok_rows, -1)
        added = jnp.concatenate([from_offset(sent[k], "core", CORES, 1) for k in range(lines)])
        total = (project(near) + added.astype(jnp.float32)).astype(jnp.bfloat16)
        home = list(total.reshape(lines, tok_rows, -1))
        if lines == 4:
            joined = home[2].astype(jnp.float32) + across(home.pop(), lines, 1).astype(jnp.float32)
            home[2] = joined.astype(jnp.bfloat16)
        parts.append([across(home[m], lines, m) for m in range(len(home))])
    return final(lines, lo[None], mixed, parts)


def solution(mesh):
    dp, expert = mesh.shape["dp"], mesh.shape["expert"]
    lines = 4 if dp % 4 == 0 else 2 if dp % 2 == 0 else 1
    sizes = {"line": lines, "lo": dp // lines, "ex": expert // CORES, "core": CORES}
    inner = Mesh(mesh.devices.reshape(tuple(sizes.values())), tuple(sizes))
    rows = P(("line", "lo", "ex", "core"), None)
    slots = P(("ex", "core"), None, None)
    placed = (
        rows,
        P(),
        P(),
        P(),
        P(),
        slots,
        slots,
        P(),
        P(),
        rows,
        P(("ex", "core"), None, None, ("line", "lo")),
        P(("ex", "core"), None, ("line", "lo")),
    )

    def body(*arrays):
        return on_device(sizes, *arrays)

    return jax.shard_map(body, mesh=inner, in_specs=placed, out_specs=rows, check_vma=False)
```

```python
import functools

import jax
import jax.numpy as jnp
from jax import lax
from jax.experimental import pallas as pl
from jax.experimental.pallas import tpu as pltpu
from jax.sharding import Mesh
from jax.sharding import PartitionSpec as P

CORES = 2
LANES = 128
EXTRA = 16
VMEM = 56 * 2**20


def from_offset(value, axis, size, offset):
    if offset % size == 0:
        return value
    return lax.ppermute(value, axis, [((i + offset) % size, i) for i in range(size)])


def together(*values):
    return lax.optimization_barrier(values)


def across(value, size, mask):
    return lax.ppermute(value, "line", [(i ^ mask, i) for i in range(size)]) if mask else value


def dot(a, b, rhs_dim=0):
    return lax.dot_general(a, b, (((1,), (rhs_dim,)), ((), ())), preferred_element_type=jnp.float32)


def add(a, b):
    return (a.astype(jnp.float32) + b.astype(jnp.float32)).astype(a.dtype)


def rms_norm(values, gain):
    stat = jnp.mean(values * values, axis=-1, keepdims=True)
    return values * lax.rsqrt(stat + 1e-06) * gain.astype(jnp.float32)


def whole(array):
    return pl.BlockSpec(array.shape, lambda *_: (0,) * len(array.shape))


def brief():
    return pl.CostEstimate(flops=1, transcendentals=0, bytes_accessed=1)


def front_kernel(pairs, pieces, blocks, rows, base_ref, prompts_ref, owner_ref, gain_a_ref, gain_e_ref, router_ref, *refs):
    pair_refs, refs = refs[: 2 * pairs], refs[2 * pairs :]
    piece_refs, refs = refs[:pieces], refs[pieces:]
    token_refs, refs = refs[:blocks], refs[blocks:]
    halves = 2 if blocks % 2 == 0 else 1
    mixed_ref, weight_ref, inner_refs = refs[0], refs[1], refs[2 : 2 + halves]
    downs, ups, normed = refs[2 + halves :]
    first = 0
    for p in range(pairs):
        size = pair_refs[2 * p].shape[0]
        downs[first : first + size, :] = pair_refs[2 * p][...]
        ups[first : first + size, :] = pair_refs[2 * p + 1][...]
        first += size
    for p in range(pieces):
        size = piece_refs[p].shape[1]
        downs[first : first + size, :] = piece_refs[p][0]
        ups[first : first + size, :] = piece_refs[p][1]
        first += size
    for k in range(blocks):
        floats = token_refs[k][0:rows, :].astype(jnp.float32)
        normed[k * rows : (k + 1) * rows, :] = rms_norm(floats, gain_a_ref[...]).astype(jnp.bfloat16)
    group = 2 if blocks % 2 == 0 else 1
    for g in range(0, blocks, group):
        at = [base_ref[k] + lax.broadcasted_iota(jnp.int32, (rows, 1), 0) for k in range(g, g + group)]
        at = jnp.concatenate(at)
        inside = (at >= prompts_ref[0:1, :]) & (at < prompts_ref[1:2, :])
        slot = jnp.sum(jnp.where(inside, prompts_ref[2:3, :], 0), axis=1, keepdims=True)
        low = dot(normed[g * rows : (g + group) * rows, :], downs[...], 1)
        low = jnp.where(owner_ref[...] == slot, low, 0.0).astype(jnp.bfloat16)
        delta = dot(low, ups[...])
        for k in range(g, g + group):
            floats = token_refs[k][0:rows, :].astype(jnp.float32)
            mixed = (floats + 2.0 * delta[(k - g) * rows : (k - g + 1) * rows, :]).astype(jnp.bfloat16)
            if k == 0:
                mixed_ref[...] = mixed
            inner = rms_norm(mixed.astype(jnp.float32), gain_e_ref[...]).astype(jnp.bfloat16)
            place = k % (blocks // halves) * rows
            inner_refs[k * halves // blocks][place : place + rows, :] = inner
            prob = jax.nn.sigmoid(dot(router_ref[...], inner, 1))
            expert = lax.broadcasted_iota(jnp.int32, (LANES, rows), 0).astype(jnp.float32)
            ids = token_refs[k][rows : rows + EXTRA, :].astype(jnp.float32)
            chosen = (ids[0:1, 0:rows] == expert) | (ids[1:2, 0:rows] == expert)
            weight_ref[k * rows : (k + 1) * rows, :] = jnp.where(chosen, prob, 0.0).T


def front(bases, prompts, owner, gain_a, gain_e, router, pairs, pieces, tokens):
    rows = tokens[0].shape[0] - EXTRA
    width = tokens[0].shape[1]
    blocks = len(tokens)
    outs = [
        jax.ShapeDtypeStruct((rows, width), jnp.bfloat16),
        jax.ShapeDtypeStruct((blocks * rows, LANES), jnp.float32),
    ]
    halves = 2 if blocks % 2 == 0 else 1
    outs += [jax.ShapeDtypeStruct((blocks * rows // halves, width), jnp.bfloat16)] * halves
    arrays = [prompts, owner, gain_a, gain_e, router, *pairs, *pieces, *tokens]
    total = owner.shape[1]
    scratch = [pltpu.VMEM((n, width), jnp.bfloat16) for n in (total, total, blocks * rows)]
    mixed, weight, *inner = pl.pallas_call(
        functools.partial(front_kernel, len(pairs) // 2, len(pieces), blocks, rows),
        grid=(1,),
        out_shape=outs,
        in_specs=[pl.BlockSpec(memory_space=pltpu.SMEM)] + [whole(a) for a in arrays],
        out_specs=[whole(a) for a in outs],
        scratch_shapes=scratch,
        compiler_params=pltpu.CompilerParams(vmem_limit_bytes=VMEM),
        cost_estimate=brief(),
        name="front",
    )(bases, *arrays)
    return mixed, weight, inner


def hidden_kernel(los, tiles, at_ref, *refs):
    x_refs, refs = refs[:tiles], refs[tiles:]
    weight_ref, gate_refs, up_refs = refs[0], refs[1 : 1 + los], refs[1 + los : 1 + 2 * los]
    act_ref, gate, up = refs[1 + 2 * los :]
    units = gate_refs[0].shape[0]

    @pl.when(pl.program_id(0) == 0)
    def _():
        for j in range(los):
            place = pl.ds(pl.multiple_of(lax.rem(at_ref[1] + j, los) * units, 16), units)
            gate[place, :] = gate_refs[j][...]
            up[place, :] = up_refs[j][...]

    for t in range(tiles):

        def work(t=t):
            x = x_refs[t][...]
            lane = lax.broadcasted_iota(jnp.int32, (x.shape[0], LANES), 1)
            scale = jnp.sum(jnp.where(lane == at_ref[0], weight_ref[...], 0.0), axis=1, keepdims=True)
            gated = jax.nn.gelu(dot(x, gate[...], 1), approximate=True)
            act_ref[...] = (gated * dot(x, up[...], 1) * scale).astype(jnp.bfloat16)

        pl.when(pl.program_id(0) == t)(work)


def hidden(at, xs, weight, gates, ups):
    tiles, (tile, width) = len(xs), xs[0].shape
    los, units = len(gates), gates[0].shape[0]
    return pl.pallas_call(
        functools.partial(hidden_kernel, los, tiles),
        grid=(tiles,),
        out_shape=jax.ShapeDtypeStruct((tiles * tile, los * units), jnp.bfloat16),
        in_specs=[pl.BlockSpec(memory_space=pltpu.SMEM)]
        + [whole(x) for x in xs]
        + [pl.BlockSpec((tile, LANES), lambda i: (i, 0))]
        + [whole(a) for a in (*gates, *ups)],
        out_specs=pl.BlockSpec((tile, los * units), lambda i: (i, 0)),
        scratch_shapes=[pltpu.VMEM((los * units, width), jnp.bfloat16)] * 2,
        compiler_params=pltpu.CompilerParams(vmem_limit_bytes=VMEM // 2),
        cost_estimate=brief(),
        name="hidden",
    )(at, *xs, weight, *gates, *ups)


def project_kernel(exs, lines, has_added, *refs):
    act_refs, down_refs, refs = refs[:exs], refs[exs : 2 * exs], refs[2 * exs :]
    added_refs, out_refs = (refs[:lines], refs[lines:]) if has_added else (None, refs)
    total = dot(act_refs[0][...], down_refs[0][...])
    for i in range(1, exs):
        total = total + dot(act_refs[i][...], down_refs[i][...])
    for k in range(lines):

        def store(k=k):
            value = total + added_refs[k][...].astype(jnp.float32) if has_added else total
            out_refs[k][...] = value.astype(jnp.bfloat16)

        pl.when(pl.program_id(0) == k)(store)


def project(lines, acts, downs, added):
    units, cols = downs[0].shape
    rows = acts[0].shape[0] // lines
    block = jax.ShapeDtypeStruct((rows, cols), jnp.bfloat16)
    return pl.pallas_call(
        functools.partial(project_kernel, len(acts), lines, bool(added)),
        grid=(lines,),
        out_shape=[block] * lines,
        in_specs=[pl.BlockSpec((rows, units), lambda i: (i, 0))] * len(acts) + [whole(a) for a in (*downs, *added)],
        out_specs=[whole(block)] * lines,
        compiler_params=pltpu.CompilerParams(vmem_limit_bytes=VMEM // 3),
        cost_estimate=brief(),
        name="project",
    )(*acts, *downs, *added)


def final_kernel(los, lines, count, lo_ref, mixed_ref, *refs):
    out_ref = refs[-1]
    cols = mixed_ref.shape[1] // (los * lines)
    for j in range(los):
        parts = refs[j * count : (j + 1) * count]
        total = parts[0][...].astype(jnp.float32)
        for part in parts[1:]:
            total = total + part[...].astype(jnp.float32)
        for h in range(lines):
            first = (h * los + lax.rem(lo_ref[0] + j, los)) * cols
            place = pl.ds(pl.multiple_of(first, LANES), cols)
            own = mixed_ref[:, place].astype(jnp.float32)
            out_ref[:, place] = (own + total[:, h * cols : (h + 1) * cols]).astype(jnp.bfloat16)


def final(lines, lo, mixed, parts):
    los, count = len(parts), len(parts[0])
    rows, width = mixed.shape
    if width // (los * lines) % LANES:
        sums = [sum(p.astype(jnp.float32) for p in group).reshape(rows, lines, -1) for group in parts]
        total = jnp.roll(jnp.stack(sums, axis=2), lo[0], axis=2).reshape(rows, width)
        return (mixed.astype(jnp.float32) + total).astype(jnp.bfloat16)
    flat = [p for group in parts for p in group]
    return pl.pallas_call(
        functools.partial(final_kernel, los, lines, count),
        out_shape=jax.ShapeDtypeStruct(mixed.shape, jnp.bfloat16),
        grid=(1,),
        in_specs=[pl.BlockSpec(memory_space=pltpu.SMEM)] + [whole(a) for a in (mixed, *flat)],
        out_specs=whole(mixed),
        compiler_params=pltpu.CompilerParams(vmem_limit_bytes=VMEM // 4),
        cost_estimate=brief(),
        name="final",
    )(lo, mixed, *flat)


def on_device(
    sizes,
    residual_input,
    prompt_token_length,
    prompt_adapter_index,
    adapter_table_row,
    adapter_norm_gain,
    adapter_down_maps,
    adapter_up_maps,
    expert_norm_gain,
    router,
    token_expert_index,
    expert_gate_up_weight,
    expert_down_weight,
):
    lines, los, exs = sizes["line"], sizes["lo"], sizes["ex"]
    tok_rows, width = residual_input.shape
    num_experts = router.shape[1]
    line, lo, ex, core = (lax.axis_index(n) for n in ("line", "lo", "ex", "core"))

    down_rows = expert_down_weight.shape[1]
    cols = expert_down_weight.shape[2]
    slots, rank, _ = adapter_down_maps.shape
    shares = los if slots % los == 0 else 1
    share = slots // shares
    ex_far, lo_far = range(1, exs), range(1, los)

    ids = token_expert_index.T.astype(jnp.bfloat16)
    ids = jnp.pad(ids, ((0, EXTRA - ids.shape[0]), (0, width - tok_rows)))
    block = jnp.concatenate([residual_input, ids])
    maps = [m.reshape(slots * rank, width) for m in (adapter_down_maps, adapter_up_maps)]
    first = lo * share * rank if shares > 1 else 0
    sent = lax.dynamic_slice_in_dim(jnp.stack(maps), first, share * rank, axis=1)
    crossed = [from_offset(sent, "ex", exs, i) for i in ex_far]
    gate, up = expert_gate_up_weight[0, 0].T, expert_gate_up_weight[0, 1].T
    ups = {(0, j): from_offset(up, "lo", los, j) for j in lo_far}
    tokens = {m: across(block, lines, m) for m in (2, 1, 0) if m < lines}
    other_maps = [from_offset(m, "core", CORES, 1) for m in maps]

    ends = jnp.cumsum(prompt_token_length)
    adapter_ids = jnp.arange(adapter_table_row.shape[0], dtype=jnp.int32)
    named = prompt_adapter_index[:, None] == adapter_ids[None, :]
    prompt_row = jnp.sum(jnp.where(named, adapter_table_row[None, :], 0), axis=1)
    prompts = jnp.stack([ends - prompt_token_length, ends, prompt_row])
    router_rows = jnp.pad(router.T, ((0, LANES - num_experts), (0, 0)))
    offsets = line ^ jnp.arange(lines, dtype=jnp.int32)
    bases = (((offsets * los + lo) * exs + ex) * CORES + core) * tok_rows
    number = jnp.arange(slots * rank, dtype=jnp.int32) // rank
    both = lambda slot: [slot, slot + jnp.where(core == 0, slots, -slots)]
    owners = both((ex * CORES + core) * slots + number)
    for i in ex_far:
        for j in range(shares):
            start = ((ex + i) % exs * CORES + core) * slots + (lo + j) % los * share
            owners += both(start + number[: share * rank])
    owner = jnp.concatenate(owners)[None, :]
    small = [bases, prompts, owner, adapter_norm_gain[None], expert_norm_gain[None], router_rows]

    gate, up, small, crossed, ups, tokens, other_maps = together(gate, up, small, crossed, ups, tokens, other_maps)
    passed = [from_offset(c, "lo", los, j) for c in crossed for j in range(shares)]
    gates = {(i, 0): from_offset(gate, "ex", exs, i) for i in ex_far}
    if lines == 4:
        tokens[3] = across(tokens[2], lines, 1)

    gate, up, passed, gates, tokens, down = together(gate, up, passed, gates, tokens, expert_down_weight)
    down = lax.all_to_all(
        down.reshape(lines, down_rows // lines, cols), "line", split_axis=0, concat_axis=0, tiled=True
    )
    held = [v for p in passed for v in (p, from_offset(p, "core", CORES, 1))]
    held, tokens, gate, up = together(held, tokens, gate, up)
    gates.update({(0, j): from_offset(gate, "lo", los, j) for j in lo_far})
    ups.update({(i, 0): from_offset(up, "ex", exs, i) for i in ex_far})
    mixed, w_own, x_own = front(*small, maps + other_maps, held, [tokens[m] for m in range(lines)])

    gates, ups, gate, up, x_own, w_own = together(gates, ups, gate, up, x_own, w_own)
    gates[0, 0], ups[0, 0] = gate, up
    for i in ex_far:
        for j in lo_far:
            gates[i, j] = from_offset(gates[i, 0], "lo", los, j)
            ups[i, j] = from_offset(ups[0, j], "ex", exs, i)
    x_far = [from_offset(v, "core", CORES, 1) for v in x_own]
    w_far = from_offset(w_own, "core", CORES, 1)

    def act(i, x, w):
        at = jnp.stack([(ex + i) % exs * CORES + core, lo])
        return hidden(at, x, w, *([of[i, j] for j in range(los)] for of in (gates, ups)))

    near, far = [act(0, x_own, w_own)], [act(0, x_far, w_far)]
    down = down.transpose(1, 0, 2).reshape(down_rows // lines, lines * cols)
    downs = {(i, 0): from_offset(down, "ex", exs, i) for i in range(exs)}
    downs.update({(0, j): from_offset(down, "lo", los, j) for j in lo_far})
    places = [(a, b) for a in range(los) for b in range(exs)]
    for i in ex_far:
        for j in lo_far:
            moves = [((a + j) % los * exs + (b + i) % exs, a * exs + b) for a, b in places]
            downs[i, j] = lax.ppermute(down, ("lo", "ex"), moves)

    x_own, w_own, x_far, w_far, near, far, gates, ups = together(x_own, w_own, x_far, w_far, near, far, gates, ups)
    far += [act(i, x_far, w_far) for i in ex_far]
    near += [act(i, x_own, w_own) for i in ex_far]

    direct = [(i, 0) for i in range(exs)] + [(0, j) for j in lo_far]
    near, far, pieces = together(near, far, [downs[k] for k in direct])
    downs.update(zip(direct, pieces))
    parts = []
    joined = None
    for j in range(los):
        of_piece = [downs[i, j] for i in range(exs)]
        if joined is not None:
            near, far, of_piece, joined = together(near, far, of_piece, joined)
            parts[-1].append(across(joined, lines, 2))
        if j == 0:
            sums = lambda acts: sum(dot(a, d) for a, d in zip(acts, of_piece))
            sent = sums(far).astype(jnp.bfloat16).reshape(lines, tok_rows, -1)
            added = jnp.concatenate([from_offset(sent[k], "core", CORES, 1) for k in range(lines)])
            total = (sums(near) + added.astype(jnp.float32)).astype(jnp.bfloat16)
            home = list(total.reshape(lines, tok_rows, -1))
        else:
            sent = project(lines, far, of_piece, [])
            home = project(lines, near, of_piece, [from_offset(v, "core", CORES, 1) for v in sent])
        if lines == 4:
            passing = across(home[3], lines, 1)
            if j > 0:
                passing, parts[-1] = together(passing, parts[-1])
            joined = add(home[2], passing)
            parts.append([home[0], across(home[1], lines, 1)])
        else:
            parts.append([across(home[m], lines, m) for m in range(lines)])
    if lines == 4:
        parts[-1].append(across(joined, lines, 2))
    return final(lines, lo[None], mixed, parts)


def solution(mesh):
    dp, expert = mesh.shape["dp"], mesh.shape["expert"]
    lines = 4 if dp % 4 == 0 else 2 if dp % 2 == 0 else 1
    sizes = {"line": lines, "lo": dp // lines, "ex": expert // CORES, "core": CORES}
    inner = Mesh(mesh.devices.reshape(tuple(sizes.values())), tuple(sizes))
    rows = P(("line", "lo", "ex", "core"), None)
    slots = P(("ex", "core"), None, None)
    placed = (
        rows,
        P(),
        P(),
        P(),
        P(),
        slots,
        slots,
        P(),
        P(),
        rows,
        P(("ex", "core"), None, None, ("line", "lo")),
        P(("ex", "core"), None, ("line", "lo")),
    )

    def body(*arrays):
        return on_device(sizes, *arrays)

    return jax.shard_map(body, mesh=inner, in_specs=placed, out_specs=rows, check_vma=False)
```

```python
import functools

import jax
import jax.numpy as jnp
from jax import lax
from jax.experimental import pallas as pl
from jax.experimental.pallas import tpu as pltpu
from jax.sharding import Mesh
from jax.sharding import PartitionSpec as P

CORES = 2
LANES = 128
EXTRA = 16
VMEM = 56 * 2**20


def from_offset(value, axis, size, offset):
    if offset % size == 0:
        return value
    return lax.ppermute(value, axis, [((i + offset) % size, i) for i in range(size)])


def together(*values):
    return lax.optimization_barrier(values)


def across(value, size, mask):
    return lax.ppermute(value, "line", [(i ^ mask, i) for i in range(size)]) if mask else value


def dot(a, b, rhs_dim=0):
    return lax.dot_general(a, b, (((1,), (rhs_dim,)), ((), ())), preferred_element_type=jnp.float32)


def add(a, b):
    return (a.astype(jnp.float32) + b.astype(jnp.float32)).astype(a.dtype)


def rms_norm(values, gain):
    stat = jnp.mean(values * values, axis=-1, keepdims=True)
    return values * lax.rsqrt(stat + 1e-06) * gain.astype(jnp.float32)


def whole(array):
    return pl.BlockSpec(array.shape, lambda *_: (0,) * len(array.shape))


def brief():
    return pl.CostEstimate(flops=1, transcendentals=0, bytes_accessed=1)


def front_kernel(pairs, pieces, blocks, rows, base_ref, prompts_ref, owner_ref, gain_a_ref, gain_e_ref, router_ref, *refs):
    pair_refs, refs = refs[: 2 * pairs], refs[2 * pairs :]
    piece_refs, refs = refs[:pieces], refs[pieces:]
    token_refs, refs = refs[:blocks], refs[blocks:]
    halves = 2 if blocks % 2 == 0 else 1
    mixed_ref, weight_ref, inner_refs = refs[0], refs[1], refs[2 : 2 + halves]
    downs, ups, normed = refs[2 + halves :]
    first = 0
    for p in range(pairs):
        size = pair_refs[2 * p].shape[0]
        downs[first : first + size, :] = pair_refs[2 * p][...]
        ups[first : first + size, :] = pair_refs[2 * p + 1][...]
        first += size
    for p in range(pieces):
        size = piece_refs[p].shape[1]
        downs[first : first + size, :] = piece_refs[p][0]
        ups[first : first + size, :] = piece_refs[p][1]
        first += size
    for k in range(blocks):
        floats = token_refs[k][0:rows, :].astype(jnp.float32)
        normed[k * rows : (k + 1) * rows, :] = rms_norm(floats, gain_a_ref[...]).astype(jnp.bfloat16)
    group = 2 if blocks % 2 == 0 else 1
    for g in range(0, blocks, group):
        at = [base_ref[k] + lax.broadcasted_iota(jnp.int32, (rows, 1), 0) for k in range(g, g + group)]
        at = jnp.concatenate(at)
        inside = (at >= prompts_ref[0:1, :]) & (at < prompts_ref[1:2, :])
        slot = jnp.sum(jnp.where(inside, prompts_ref[2:3, :], 0), axis=1, keepdims=True)
        low = dot(normed[g * rows : (g + group) * rows, :], downs[...], 1)
        low = jnp.where(owner_ref[...] == slot, low, 0.0).astype(jnp.bfloat16)
        delta = dot(low, ups[...])
        for k in range(g, g + group):
            floats = token_refs[k][0:rows, :].astype(jnp.float32)
            mixed = (floats + 2.0 * delta[(k - g) * rows : (k - g + 1) * rows, :]).astype(jnp.bfloat16)
            if k == 0:
                mixed_ref[...] = mixed
            inner = rms_norm(mixed.astype(jnp.float32), gain_e_ref[...]).astype(jnp.bfloat16)
            place = k % (blocks // halves) * rows
            inner_refs[k * halves // blocks][place : place + rows, :] = inner
            prob = jax.nn.sigmoid(dot(router_ref[...], inner, 1))
            expert = lax.broadcasted_iota(jnp.int32, (LANES, rows), 0).astype(jnp.float32)
            ids = token_refs[k][rows : rows + EXTRA, :].astype(jnp.float32)
            chosen = (ids[0:1, 0:rows] == expert) | (ids[1:2, 0:rows] == expert)
            weight_ref[k * rows : (k + 1) * rows, :] = jnp.where(chosen, prob, 0.0).T


def front(bases, prompts, owner, gain_a, gain_e, router, pairs, pieces, tokens):
    rows = tokens[0].shape[0] - EXTRA
    width = tokens[0].shape[1]
    blocks = len(tokens)
    outs = [
        jax.ShapeDtypeStruct((rows, width), jnp.bfloat16),
        jax.ShapeDtypeStruct((blocks * rows, LANES), jnp.float32),
    ]
    halves = 2 if blocks % 2 == 0 else 1
    outs += [jax.ShapeDtypeStruct((blocks * rows // halves, width), jnp.bfloat16)] * halves
    arrays = [prompts, owner, gain_a, gain_e, router, *pairs, *pieces, *tokens]
    total = owner.shape[1]
    scratch = [pltpu.VMEM((n, width), jnp.bfloat16) for n in (total, total, blocks * rows)]
    mixed, weight, *inner = pl.pallas_call(
        functools.partial(front_kernel, len(pairs) // 2, len(pieces), blocks, rows),
        grid=(1,),
        out_shape=outs,
        in_specs=[pl.BlockSpec(memory_space=pltpu.SMEM)] + [whole(a) for a in arrays],
        out_specs=[whole(a) for a in outs],
        scratch_shapes=scratch,
        compiler_params=pltpu.CompilerParams(vmem_limit_bytes=VMEM),
        cost_estimate=brief(),
        name="front",
    )(bases, *arrays)
    return mixed, weight, inner


def hidden_kernel(los, tiles, at_ref, *refs):
    x_refs, refs = refs[:tiles], refs[tiles:]
    weight_ref, gate_refs, up_refs = refs[0], refs[1 : 1 + los], refs[1 + los : 1 + 2 * los]
    act_ref, gate, up = refs[1 + 2 * los :]
    units = gate_refs[0].shape[0]

    @pl.when(pl.program_id(0) == 0)
    def _():
        for j in range(los):
            place = pl.ds(pl.multiple_of(lax.rem(at_ref[1] + j, los) * units, 16), units)
            gate[place, :] = gate_refs[j][...]
            up[place, :] = up_refs[j][...]

    for t in range(tiles):

        def work(t=t):
            x = x_refs[t][...]
            lane = lax.broadcasted_iota(jnp.int32, (x.shape[0], LANES), 1)
            scale = jnp.sum(jnp.where(lane == at_ref[0], weight_ref[...], 0.0), axis=1, keepdims=True)
            gated = jax.nn.gelu(dot(x, gate[...], 1), approximate=True)
            act_ref[...] = (gated * dot(x, up[...], 1) * scale).astype(jnp.bfloat16)

        pl.when(pl.program_id(0) == t)(work)


def hidden(at, xs, weight, gates, ups):
    tiles, (tile, width) = len(xs), xs[0].shape
    los, units = len(gates), gates[0].shape[0]
    return pl.pallas_call(
        functools.partial(hidden_kernel, los, tiles),
        grid=(tiles,),
        out_shape=jax.ShapeDtypeStruct((tiles * tile, los * units), jnp.bfloat16),
        in_specs=[pl.BlockSpec(memory_space=pltpu.SMEM)]
        + [whole(x) for x in xs]
        + [pl.BlockSpec((tile, LANES), lambda i: (i, 0))]
        + [whole(a) for a in (*gates, *ups)],
        out_specs=pl.BlockSpec((tile, los * units), lambda i: (i, 0)),
        scratch_shapes=[pltpu.VMEM((los * units, width), jnp.bfloat16)] * 2,
        compiler_params=pltpu.CompilerParams(vmem_limit_bytes=VMEM // 2),
        cost_estimate=brief(),
        name="hidden",
    )(at, *xs, weight, *gates, *ups)


def project_kernel(exs, lines, has_added, *refs):
    act_refs, down_refs, refs = refs[:exs], refs[exs : 2 * exs], refs[2 * exs :]
    added_refs, out_refs = (refs[:lines], refs[lines:]) if has_added else (None, refs)
    total = dot(act_refs[0][...], down_refs[0][...])
    for i in range(1, exs):
        total = total + dot(act_refs[i][...], down_refs[i][...])
    for k in range(lines):

        def store(k=k):
            value = total + added_refs[k][...].astype(jnp.float32) if has_added else total
            out_refs[k][...] = value.astype(jnp.bfloat16)

        pl.when(pl.program_id(0) == k)(store)


def project(lines, acts, downs, added):
    units, cols = downs[0].shape
    rows = acts[0].shape[0] // lines
    block = jax.ShapeDtypeStruct((rows, cols), jnp.bfloat16)
    return pl.pallas_call(
        functools.partial(project_kernel, len(acts), lines, bool(added)),
        grid=(lines,),
        out_shape=[block] * lines,
        in_specs=[pl.BlockSpec((rows, units), lambda i: (i, 0))] * len(acts) + [whole(a) for a in (*downs, *added)],
        out_specs=[whole(block)] * lines,
        compiler_params=pltpu.CompilerParams(vmem_limit_bytes=VMEM // 3),
        cost_estimate=brief(),
        name="project",
    )(*acts, *downs, *added)


def final_kernel(los, lines, count, lo_ref, mixed_ref, *refs):
    out_ref = refs[-1]
    cols = mixed_ref.shape[1] // (los * lines)
    for j in range(los):
        parts = refs[j * count : (j + 1) * count]
        total = parts[0][...].astype(jnp.float32)
        for part in parts[1:]:
            total = total + part[...].astype(jnp.float32)
        for h in range(lines):
            first = (h * los + lax.rem(lo_ref[0] + j, los)) * cols
            place = pl.ds(pl.multiple_of(first, LANES), cols)
            own = mixed_ref[:, place].astype(jnp.float32)
            out_ref[:, place] = (own + total[:, h * cols : (h + 1) * cols]).astype(jnp.bfloat16)


def final(lines, lo, mixed, parts):
    los, count = len(parts), len(parts[0])
    rows, width = mixed.shape
    if width // (los * lines) % LANES:
        sums = [sum(p.astype(jnp.float32) for p in group).reshape(rows, lines, -1) for group in parts]
        total = jnp.roll(jnp.stack(sums, axis=2), lo[0], axis=2).reshape(rows, width)
        return (mixed.astype(jnp.float32) + total).astype(jnp.bfloat16)
    flat = [p for group in parts for p in group]
    return pl.pallas_call(
        functools.partial(final_kernel, los, lines, count),
        out_shape=jax.ShapeDtypeStruct(mixed.shape, jnp.bfloat16),
        grid=(1,),
        in_specs=[pl.BlockSpec(memory_space=pltpu.SMEM)] + [whole(a) for a in (mixed, *flat)],
        out_specs=whole(mixed),
        compiler_params=pltpu.CompilerParams(vmem_limit_bytes=VMEM // 4),
        cost_estimate=brief(),
        name="final",
    )(lo, mixed, *flat)


def on_device(
    sizes,
    residual_input,
    prompt_token_length,
    prompt_adapter_index,
    adapter_table_row,
    adapter_norm_gain,
    adapter_down_maps,
    adapter_up_maps,
    expert_norm_gain,
    router,
    token_expert_index,
    expert_gate_up_weight,
    expert_down_weight,
):
    lines, los, exs = sizes["line"], sizes["lo"], sizes["ex"]
    tok_rows, width = residual_input.shape
    num_experts = router.shape[1]
    line, lo, ex, core = (lax.axis_index(n) for n in ("line", "lo", "ex", "core"))

    down_rows = expert_down_weight.shape[1]
    cols = expert_down_weight.shape[2]
    slots, rank, _ = adapter_down_maps.shape
    shares = los if slots % los == 0 else 1
    share = slots // shares
    ex_far, lo_far = range(1, exs), range(1, los)

    ids = token_expert_index.T.astype(jnp.bfloat16)
    ids = jnp.pad(ids, ((0, EXTRA - ids.shape[0]), (0, width - tok_rows)))
    block = jnp.concatenate([residual_input, ids])
    maps = [m.reshape(slots * rank, width) for m in (adapter_down_maps, adapter_up_maps)]
    first = lo * share * rank if shares > 1 else 0
    sent = lax.dynamic_slice_in_dim(jnp.stack(maps), first, share * rank, axis=1)
    crossed = [from_offset(sent, "ex", exs, i) for i in ex_far]
    gate, up = expert_gate_up_weight[0, 0].T, expert_gate_up_weight[0, 1].T
    ups = {(0, j): from_offset(up, "lo", los, j) for j in lo_far}
    tokens = {m: across(block, lines, m) for m in (2, 1, 0) if m < lines}
    other_maps = [from_offset(m, "core", CORES, 1) for m in maps]

    ends = jnp.cumsum(prompt_token_length)
    adapter_ids = jnp.arange(adapter_table_row.shape[0], dtype=jnp.int32)
    named = prompt_adapter_index[:, None] == adapter_ids[None, :]
    prompt_row = jnp.sum(jnp.where(named, adapter_table_row[None, :], 0), axis=1)
    prompts = jnp.stack([ends - prompt_token_length, ends, prompt_row])
    router_rows = jnp.pad(router.T, ((0, LANES - num_experts), (0, 0)))
    offsets = line ^ jnp.arange(lines, dtype=jnp.int32)
    bases = (((offsets * los + lo) * exs + ex) * CORES + core) * tok_rows
    number = jnp.arange(slots * rank, dtype=jnp.int32) // rank
    both = lambda slot: [slot, slot + jnp.where(core == 0, slots, -slots)]
    owners = both((ex * CORES + core) * slots + number)
    for i in ex_far:
        for j in range(shares):
            start = ((ex + i) % exs * CORES + core) * slots + (lo + j) % los * share
            owners += both(start + number[: share * rank])
    owner = jnp.concatenate(owners)[None, :]
    small = [bases, prompts, owner, adapter_norm_gain[None], expert_norm_gain[None], router_rows]

    passed = [from_offset(c, "lo", los, j) for c in crossed for j in range(shares)]
    gate, up, small, ups, tokens, other_maps = together(gate, up, small, ups, tokens, other_maps)
    gates = {(i, 0): from_offset(gate, "ex", exs, i) for i in ex_far}
    if lines == 4:
        tokens[3] = across(tokens[2], lines, 1)
    held = [v for p in passed for v in (p, from_offset(p, "core", CORES, 1))]

    gates, tokens, held, gate, up, down = together(gates, tokens, held, gate, up, expert_down_weight)
    gates.update({(0, j): from_offset(gate, "lo", los, j) for j in lo_far})
    ups.update({(i, 0): from_offset(up, "ex", exs, i) for i in ex_far})
    down = lax.all_to_all(
        down.reshape(lines, down_rows // lines, cols), "line", split_axis=0, concat_axis=0, tiled=True
    )
    mixed, w_own, x_own = front(*small, maps + other_maps, held, [tokens[m] for m in range(lines)])

    gates, ups, gate, up, x_own, w_own = together(gates, ups, gate, up, x_own, w_own)
    gates[0, 0], ups[0, 0] = gate, up
    for i in ex_far:
        for j in lo_far:
            gates[i, j] = from_offset(gates[i, 0], "lo", los, j)
            ups[i, j] = from_offset(ups[0, j], "ex", exs, i)
    x_far = [from_offset(v, "core", CORES, 1) for v in x_own]
    w_far = from_offset(w_own, "core", CORES, 1)

    def act(i, x, w):
        at = jnp.stack([(ex + i) % exs * CORES + core, lo])
        return hidden(at, x, w, *([of[i, j] for j in range(los)] for of in (gates, ups)))

    near, far = [act(0, x_own, w_own)], [act(0, x_far, w_far)]
    down = down.transpose(1, 0, 2).reshape(down_rows // lines, lines * cols)
    downs = {(i, 0): from_offset(down, "ex", exs, i) for i in range(exs)}
    downs.update({(0, j): from_offset(down, "lo", los, j) for j in lo_far})
    places = [(a, b) for a in range(los) for b in range(exs)]
    for i in ex_far:
        for j in lo_far:
            moves = [((a + j) % los * exs + (b + i) % exs, a * exs + b) for a, b in places]
            downs[i, j] = lax.ppermute(down, ("lo", "ex"), moves)

    x_own, w_own, x_far, w_far, near, far, gates, ups = together(x_own, w_own, x_far, w_far, near, far, gates, ups)
    far += [act(i, x_far, w_far) for i in ex_far]
    near += [act(i, x_own, w_own) for i in ex_far]

    direct = [(i, 0) for i in range(exs)] + [(0, j) for j in lo_far]
    near, far, pieces = together(near, far, [downs[k] for k in direct])
    downs.update(zip(direct, pieces))
    parts = []
    joined = None
    for j in range(los):
        of_piece = [downs[i, j] for i in range(exs)]
        if joined is not None:
            near, far, of_piece, joined = together(near, far, of_piece, joined)
            parts[-1].append(across(joined, lines, 2))
        if j == 0:
            sums = lambda acts: sum(dot(a, d) for a, d in zip(acts, of_piece))
            sent = sums(far).astype(jnp.bfloat16).reshape(lines, tok_rows, -1)
            added = jnp.concatenate([from_offset(sent[k], "core", CORES, 1) for k in range(lines)])
            total = (sums(near) + added.astype(jnp.float32)).astype(jnp.bfloat16)
            home = list(total.reshape(lines, tok_rows, -1))
        else:
            sent = project(lines, far, of_piece, [])
            home = project(lines, near, of_piece, [from_offset(v, "core", CORES, 1) for v in sent])
        if lines == 4:
            passing = across(home[3], lines, 1)
            if j > 0:
                passing, parts[-1] = together(passing, parts[-1])
            joined = add(home[2], passing)
            parts.append([home[0], across(home[1], lines, 1)])
        else:
            parts.append([across(home[m], lines, m) for m in range(lines)])
    if lines == 4:
        parts[-1].append(across(joined, lines, 2))
    return final(lines, lo[None], mixed, parts)


def solution(mesh):
    dp, expert = mesh.shape["dp"], mesh.shape["expert"]
    lines = 4 if dp % 4 == 0 else 2 if dp % 2 == 0 else 1
    sizes = {"line": lines, "lo": dp // lines, "ex": expert // CORES, "core": CORES}
    inner = Mesh(mesh.devices.reshape(tuple(sizes.values())), tuple(sizes))
    rows = P(("line", "lo", "ex", "core"), None)
    slots = P(("ex", "core"), None, None)
    placed = (
        rows,
        P(),
        P(),
        P(),
        P(),
        slots,
        slots,
        P(),
        P(),
        rows,
        P(("ex", "core"), None, None, ("line", "lo")),
        P(("ex", "core"), None, ("line", "lo")),
    )

    def body(*arrays):
        return on_device(sizes, *arrays)

    return jax.shard_map(body, mesh=inner, in_specs=placed, out_specs=rows, check_vma=False)
```

```python
import functools

import jax
import jax.numpy as jnp
from jax import lax
from jax.experimental import pallas as pl
from jax.experimental.pallas import tpu as pltpu
from jax.sharding import Mesh
from jax.sharding import PartitionSpec as P

CORES = 2
LANES = 128
EXTRA = 16
VMEM = 56 * 2**20


def from_offset(value, axis, size, offset):
    if offset % size == 0:
        return value
    return lax.ppermute(value, axis, [((i + offset) % size, i) for i in range(size)])


def together(*values):
    return lax.optimization_barrier(values)


def across(value, size, mask):
    return lax.ppermute(value, "line", [(i ^ mask, i) for i in range(size)]) if mask else value


def dot(a, b, rhs_dim=0):
    return lax.dot_general(a, b, (((1,), (rhs_dim,)), ((), ())), preferred_element_type=jnp.float32)


def add(a, b):
    return (a.astype(jnp.float32) + b.astype(jnp.float32)).astype(a.dtype)


def rms_norm(values, gain):
    stat = jnp.mean(values * values, axis=-1, keepdims=True)
    return values * lax.rsqrt(stat + 1e-06) * gain.astype(jnp.float32)


def whole(array):
    return pl.BlockSpec(array.shape, lambda *_: (0,) * len(array.shape))


def brief():
    return pl.CostEstimate(flops=1, transcendentals=0, bytes_accessed=1)


def front_kernel(pairs, pieces, blocks, rows, base_ref, prompts_ref, owner_ref, gain_a_ref, gain_e_ref, router_ref, *refs):
    pair_refs, refs = refs[: 2 * pairs], refs[2 * pairs :]
    piece_refs, refs = refs[:pieces], refs[pieces:]
    token_refs, refs = refs[:blocks], refs[blocks:]
    halves = 2 if blocks % 2 == 0 else 1
    mixed_ref, weight_ref, inner_refs = refs[0], refs[1], refs[2 : 2 + halves]
    downs, ups, normed = refs[2 + halves :]
    first = 0
    for p in range(pairs):
        size = pair_refs[2 * p].shape[0]
        downs[first : first + size, :] = pair_refs[2 * p][...]
        ups[first : first + size, :] = pair_refs[2 * p + 1][...]
        first += size
    for p in range(pieces):
        size = piece_refs[p].shape[1]
        downs[first : first + size, :] = piece_refs[p][0]
        ups[first : first + size, :] = piece_refs[p][1]
        first += size
    for k in range(blocks):
        floats = token_refs[k][0:rows, :].astype(jnp.float32)
        normed[k * rows : (k + 1) * rows, :] = rms_norm(floats, gain_a_ref[...]).astype(jnp.bfloat16)
    group = 2 if blocks % 2 == 0 else 1
    for g in range(0, blocks, group):
        at = [base_ref[k] + lax.broadcasted_iota(jnp.int32, (rows, 1), 0) for k in range(g, g + group)]
        at = jnp.concatenate(at)
        inside = (at >= prompts_ref[0:1, :]) & (at < prompts_ref[1:2, :])
        slot = jnp.sum(jnp.where(inside, prompts_ref[2:3, :], 0), axis=1, keepdims=True)
        low = dot(normed[g * rows : (g + group) * rows, :], downs[...], 1)
        low = jnp.where(owner_ref[...] == slot, low, 0.0).astype(jnp.bfloat16)
        delta = dot(low, ups[...])
        for k in range(g, g + group):
            floats = token_refs[k][0:rows, :].astype(jnp.float32)
            mixed = (floats + 2.0 * delta[(k - g) * rows : (k - g + 1) * rows, :]).astype(jnp.bfloat16)
            if k == 0:
                mixed_ref[...] = mixed
            inner = rms_norm(mixed.astype(jnp.float32), gain_e_ref[...]).astype(jnp.bfloat16)
            place = k % (blocks // halves) * rows
            inner_refs[k * halves // blocks][place : place + rows, :] = inner
            prob = jax.nn.sigmoid(dot(router_ref[...], inner, 1))
            expert = lax.broadcasted_iota(jnp.int32, (LANES, rows), 0).astype(jnp.float32)
            ids = token_refs[k][rows : rows + EXTRA, :].astype(jnp.float32)
            chosen = (ids[0:1, 0:rows] == expert) | (ids[1:2, 0:rows] == expert)
            weight_ref[k * rows : (k + 1) * rows, :] = jnp.where(chosen, prob, 0.0).T


def front(bases, prompts, owner, gain_a, gain_e, router, pairs, pieces, tokens):
    rows = tokens[0].shape[0] - EXTRA
    width = tokens[0].shape[1]
    blocks = len(tokens)
    outs = [
        jax.ShapeDtypeStruct((rows, width), jnp.bfloat16),
        jax.ShapeDtypeStruct((blocks * rows, LANES), jnp.float32),
    ]
    halves = 2 if blocks % 2 == 0 else 1
    outs += [jax.ShapeDtypeStruct((blocks * rows // halves, width), jnp.bfloat16)] * halves
    arrays = [prompts, owner, gain_a, gain_e, router, *pairs, *pieces, *tokens]
    total = owner.shape[1]
    scratch = [pltpu.VMEM((n, width), jnp.bfloat16) for n in (total, total, blocks * rows)]
    mixed, weight, *inner = pl.pallas_call(
        functools.partial(front_kernel, len(pairs) // 2, len(pieces), blocks, rows),
        grid=(1,),
        out_shape=outs,
        in_specs=[pl.BlockSpec(memory_space=pltpu.SMEM)] + [whole(a) for a in arrays],
        out_specs=[whole(a) for a in outs],
        scratch_shapes=scratch,
        compiler_params=pltpu.CompilerParams(vmem_limit_bytes=VMEM),
        cost_estimate=brief(),
        name="front",
    )(bases, *arrays)
    return mixed, weight, inner


def hidden_kernel(los, tiles, at_ref, *refs):
    x_refs, refs = refs[:tiles], refs[tiles:]
    weight_ref, gate_refs, up_refs = refs[0], refs[1 : 1 + los], refs[1 + los : 1 + 2 * los]
    act_ref, gate, up = refs[1 + 2 * los :]
    units = gate_refs[0].shape[0]

    @pl.when(pl.program_id(0) == 0)
    def _():
        for j in range(los):
            place = pl.ds(pl.multiple_of(lax.rem(at_ref[1] + j, los) * units, 16), units)
            gate[place, :] = gate_refs[j][...]
            up[place, :] = up_refs[j][...]

    for t in range(tiles):

        def work(t=t):
            x = x_refs[t][...]
            lane = lax.broadcasted_iota(jnp.int32, (x.shape[0], LANES), 1)
            scale = jnp.sum(jnp.where(lane == at_ref[0], weight_ref[...], 0.0), axis=1, keepdims=True)
            gated = jax.nn.gelu(dot(x, gate[...], 1), approximate=True)
            act_ref[...] = (gated * dot(x, up[...], 1) * scale).astype(jnp.bfloat16)

        pl.when(pl.program_id(0) == t)(work)


def hidden(at, xs, weight, gates, ups):
    tiles, (tile, width) = len(xs), xs[0].shape
    los, units = len(gates), gates[0].shape[0]
    return pl.pallas_call(
        functools.partial(hidden_kernel, los, tiles),
        grid=(tiles,),
        out_shape=jax.ShapeDtypeStruct((tiles * tile, los * units), jnp.bfloat16),
        in_specs=[pl.BlockSpec(memory_space=pltpu.SMEM)]
        + [whole(x) for x in xs]
        + [pl.BlockSpec((tile, LANES), lambda i: (i, 0))]
        + [whole(a) for a in (*gates, *ups)],
        out_specs=pl.BlockSpec((tile, los * units), lambda i: (i, 0)),
        scratch_shapes=[pltpu.VMEM((los * units, width), jnp.bfloat16)] * 2,
        compiler_params=pltpu.CompilerParams(vmem_limit_bytes=VMEM // 2),
        cost_estimate=brief(),
        name="hidden",
    )(at, *xs, weight, *gates, *ups)


def final_kernel(los, lines, count, lo_ref, mixed_ref, *refs):
    out_ref = refs[-1]
    cols = mixed_ref.shape[1] // (los * lines)
    for j in range(los):
        parts = refs[j * count : (j + 1) * count]
        total = parts[0][...].astype(jnp.float32)
        for part in parts[1:]:
            total = total + part[...].astype(jnp.float32)
        for h in range(lines):
            first = (h * los + lax.rem(lo_ref[0] + j, los)) * cols
            place = pl.ds(pl.multiple_of(first, LANES), cols)
            own = mixed_ref[:, place].astype(jnp.float32)
            out_ref[:, place] = (own + total[:, h * cols : (h + 1) * cols]).astype(jnp.bfloat16)


def final(lines, lo, mixed, parts):
    los, count = len(parts), len(parts[0])
    rows, width = mixed.shape
    if width // (los * lines) % LANES:
        sums = [sum(p.astype(jnp.float32) for p in group).reshape(rows, lines, -1) for group in parts]
        total = jnp.roll(jnp.stack(sums, axis=2), lo[0], axis=2).reshape(rows, width)
        return (mixed.astype(jnp.float32) + total).astype(jnp.bfloat16)
    flat = [p for group in parts for p in group]
    return pl.pallas_call(
        functools.partial(final_kernel, los, lines, count),
        out_shape=jax.ShapeDtypeStruct(mixed.shape, jnp.bfloat16),
        grid=(1,),
        in_specs=[pl.BlockSpec(memory_space=pltpu.SMEM)] + [whole(a) for a in (mixed, *flat)],
        out_specs=whole(mixed),
        compiler_params=pltpu.CompilerParams(vmem_limit_bytes=VMEM // 4),
        cost_estimate=brief(),
        name="final",
    )(lo, mixed, *flat)


def on_device(
    sizes,
    residual_input,
    prompt_token_length,
    prompt_adapter_index,
    adapter_table_row,
    adapter_norm_gain,
    adapter_down_maps,
    adapter_up_maps,
    expert_norm_gain,
    router,
    token_expert_index,
    expert_gate_up_weight,
    expert_down_weight,
):
    lines, los, exs = sizes["line"], sizes["lo"], sizes["ex"]
    tok_rows, width = residual_input.shape
    num_experts = router.shape[1]
    line, lo, ex, core = (lax.axis_index(n) for n in ("line", "lo", "ex", "core"))

    down_rows = expert_down_weight.shape[1]
    cols = expert_down_weight.shape[2]
    slots, rank, _ = adapter_down_maps.shape
    shares = los if slots % los == 0 else 1
    share = slots // shares
    ex_far, lo_far = range(1, exs), range(1, los)

    ids = token_expert_index.T.astype(jnp.bfloat16)
    ids = jnp.pad(ids, ((0, EXTRA - ids.shape[0]), (0, width - tok_rows)))
    block = jnp.concatenate([residual_input, ids])
    maps = [m.reshape(slots * rank, width) for m in (adapter_down_maps, adapter_up_maps)]
    first = lo * share * rank if shares > 1 else 0
    sent = lax.dynamic_slice_in_dim(jnp.stack(maps), first, share * rank, axis=1)
    crossed = [from_offset(sent, "ex", exs, i) for i in ex_far]
    gate, up = expert_gate_up_weight[0, 0].T, expert_gate_up_weight[0, 1].T
    ups = {(0, j): from_offset(up, "lo", los, j) for j in lo_far}
    tokens = {m: across(block, lines, m) for m in (2, 1, 0) if m < lines}
    other_maps = [from_offset(m, "core", CORES, 1) for m in maps]

    ends = jnp.cumsum(prompt_token_length)
    adapter_ids = jnp.arange(adapter_table_row.shape[0], dtype=jnp.int32)
    named = prompt_adapter_index[:, None] == adapter_ids[None, :]
    prompt_row = jnp.sum(jnp.where(named, adapter_table_row[None, :], 0), axis=1)
    prompts = jnp.stack([ends - prompt_token_length, ends, prompt_row])
    router_rows = jnp.pad(router.T, ((0, LANES - num_experts), (0, 0)))
    offsets = line ^ jnp.arange(lines, dtype=jnp.int32)
    bases = (((offsets * los + lo) * exs + ex) * CORES + core) * tok_rows
    number = jnp.arange(slots * rank, dtype=jnp.int32) // rank
    both = lambda slot: [slot, slot + jnp.where(core == 0, slots, -slots)]
    owners = both((ex * CORES + core) * slots + number)
    for i in ex_far:
        for j in range(shares):
            start = ((ex + i) % exs * CORES + core) * slots + (lo + j) % los * share
            owners += both(start + number[: share * rank])
    owner = jnp.concatenate(owners)[None, :]
    small = [bases, prompts, owner, adapter_norm_gain[None], expert_norm_gain[None], router_rows]

    passed = [from_offset(c, "lo", los, j) for c in crossed for j in range(shares)]
    gate, up, small, ups, tokens, other_maps = together(gate, up, small, ups, tokens, other_maps)
    gates = {(i, 0): from_offset(gate, "ex", exs, i) for i in ex_far}
    if lines == 4:
        tokens[3] = across(tokens[2], lines, 1)
    held = [v for p in passed for v in (p, from_offset(p, "core", CORES, 1))]

    gates, tokens, held, gate, up, down = together(gates, tokens, held, gate, up, expert_down_weight)
    gates.update({(0, j): from_offset(gate, "lo", los, j) for j in lo_far})
    ups.update({(i, 0): from_offset(up, "ex", exs, i) for i in ex_far})
    down = lax.all_to_all(
        down.reshape(lines, down_rows // lines, cols), "line", split_axis=0, concat_axis=0, tiled=True
    )
    mixed, w_own, x_own = front(*small, maps + other_maps, held, [tokens[m] for m in range(lines)])

    gates, ups, gate, up, x_own, w_own = together(gates, ups, gate, up, x_own, w_own)
    gates[0, 0], ups[0, 0] = gate, up
    for i in ex_far:
        for j in lo_far:
            gates[i, j] = from_offset(gates[i, 0], "lo", los, j)
            ups[i, j] = from_offset(ups[0, j], "ex", exs, i)
    x_far = [from_offset(v, "core", CORES, 1) for v in x_own]
    w_far = from_offset(w_own, "core", CORES, 1)

    def act(i, x, w):
        at = jnp.stack([(ex + i) % exs * CORES + core, lo])
        return hidden(at, x, w, *([of[i, j] for j in range(los)] for of in (gates, ups)))

    near, far = [act(0, x_own, w_own)], [act(0, x_far, w_far)]
    down = down.transpose(1, 0, 2).reshape(down_rows // lines, lines * cols)
    downs = {(i, 0): from_offset(down, "ex", exs, i) for i in range(exs)}
    downs.update({(0, j): from_offset(down, "lo", los, j) for j in lo_far})
    places = [(a, b) for a in range(los) for b in range(exs)]
    for i in ex_far:
        for j in lo_far:
            moves = [((a + j) % los * exs + (b + i) % exs, a * exs + b) for a, b in places]
            downs[i, j] = lax.ppermute(down, ("lo", "ex"), moves)

    x_own, w_own, x_far, w_far, near, far, gates, ups = together(x_own, w_own, x_far, w_far, near, far, gates, ups)
    far += [act(i, x_far, w_far) for i in ex_far]
    near += [act(i, x_own, w_own) for i in ex_far]

    direct = [(i, 0) for i in range(exs)] + [(0, j) for j in lo_far]
    near, far, pieces = together(near, far, [downs[k] for k in direct])
    downs.update(zip(direct, pieces))
    parts = []
    joined = None
    for j in range(los):
        of_piece = [downs[i, j] for i in range(exs)]
        if joined is not None:
            near, far, of_piece, joined = together(near, far, of_piece, joined)
            parts[-1].append(across(joined, lines, 2))
        sums = lambda acts: sum(dot(a, d) for a, d in zip(acts, of_piece))
        sent = sums(far).astype(jnp.bfloat16).reshape(lines, tok_rows, -1)
        added = jnp.concatenate([from_offset(sent[k], "core", CORES, 1) for k in range(lines)])
        total = (sums(near) + added.astype(jnp.float32)).astype(jnp.bfloat16)
        home = list(total.reshape(lines, tok_rows, -1))
        if lines == 4:
            passing = across(home[3], lines, 1)
            if j > 0:
                passing, parts[-1] = together(passing, parts[-1])
            joined = add(home[2], passing)
            parts.append([home[0], across(home[1], lines, 1)])
        else:
            parts.append([across(home[m], lines, m) for m in range(lines)])
    if lines == 4:
        parts[-1].append(across(joined, lines, 2))
    return final(lines, lo[None], mixed, parts)


def solution(mesh):
    dp, expert = mesh.shape["dp"], mesh.shape["expert"]
    lines = 4 if dp % 4 == 0 else 2 if dp % 2 == 0 else 1
    sizes = {"line": lines, "lo": dp // lines, "ex": expert // CORES, "core": CORES}
    inner = Mesh(mesh.devices.reshape(tuple(sizes.values())), tuple(sizes))
    rows = P(("line", "lo", "ex", "core"), None)
    slots = P(("ex", "core"), None, None)
    placed = (
        rows,
        P(),
        P(),
        P(),
        P(),
        slots,
        slots,
        P(),
        P(),
        rows,
        P(("ex", "core"), None, None, ("line", "lo")),
        P(("ex", "core"), None, ("line", "lo")),
    )

    def body(*arrays):
        return on_device(sizes, *arrays)

    return jax.shard_map(body, mesh=inner, in_specs=placed, out_specs=rows, check_vma=False)
```

```python
import functools

import jax
import jax.numpy as jnp
from jax import lax
from jax.experimental import pallas as pl
from jax.experimental.pallas import tpu as pltpu
from jax.sharding import Mesh
from jax.sharding import PartitionSpec as P

CORES = 2
LANES = 128
EXTRA = 16
VMEM = 56 * 2**20


def from_offset(value, axis, size, offset):
    if offset % size == 0:
        return value
    return lax.ppermute(value, axis, [((i + offset) % size, i) for i in range(size)])


def together(*values):
    return lax.optimization_barrier(values)


def across(value, size, mask):
    return lax.ppermute(value, "line", [(i ^ mask, i) for i in range(size)]) if mask else value


def dot(a, b, rhs_dim=0):
    return lax.dot_general(a, b, (((1,), (rhs_dim,)), ((), ())), preferred_element_type=jnp.float32)


def add(a, b):
    return (a.astype(jnp.float32) + b.astype(jnp.float32)).astype(a.dtype)


def rms_norm(values, gain):
    stat = jnp.mean(values * values, axis=-1, keepdims=True)
    return values * lax.rsqrt(stat + 1e-06) * gain.astype(jnp.float32)


def whole(array):
    return pl.BlockSpec(array.shape, lambda *_: (0,) * len(array.shape))


def brief():
    return pl.CostEstimate(flops=1, transcendentals=0, bytes_accessed=1)


def front_kernel(pairs, pieces, blocks, rows, base_ref, prompts_ref, owner_ref, gain_a_ref, gain_e_ref, router_ref, *refs):
    pair_refs, refs = refs[: 2 * pairs], refs[2 * pairs :]
    piece_refs, refs = refs[:pieces], refs[pieces:]
    token_refs, refs = refs[:blocks], refs[blocks:]
    halves = 2 if blocks % 2 == 0 else 1
    mixed_ref, weight_ref, inner_refs = refs[0], refs[1], refs[2 : 2 + halves]
    downs, ups, normed = refs[2 + halves :]
    first = 0
    for p in range(pairs):
        size = pair_refs[2 * p].shape[0]
        downs[first : first + size, :] = pair_refs[2 * p][...]
        ups[first : first + size, :] = pair_refs[2 * p + 1][...]
        first += size
    for p in range(pieces):
        size = piece_refs[p].shape[1]
        downs[first : first + size, :] = piece_refs[p][0]
        ups[first : first + size, :] = piece_refs[p][1]
        first += size
    for k in range(blocks):
        floats = token_refs[k][0:rows, :].astype(jnp.float32)
        normed[k * rows : (k + 1) * rows, :] = rms_norm(floats, gain_a_ref[...]).astype(jnp.bfloat16)
    group = 2 if blocks % 2 == 0 else 1
    for g in range(0, blocks, group):
        at = [base_ref[k] + lax.broadcasted_iota(jnp.int32, (rows, 1), 0) for k in range(g, g + group)]
        at = jnp.concatenate(at)
        inside = (at >= prompts_ref[0:1, :]) & (at < prompts_ref[1:2, :])
        slot = jnp.sum(jnp.where(inside, prompts_ref[2:3, :], 0), axis=1, keepdims=True)
        low = dot(normed[g * rows : (g + group) * rows, :], downs[...], 1)
        low = jnp.where(owner_ref[...] == slot, low, 0.0).astype(jnp.bfloat16)
        delta = dot(low, ups[...])
        for k in range(g, g + group):
            floats = token_refs[k][0:rows, :].astype(jnp.float32)
            mixed = (floats + 2.0 * delta[(k - g) * rows : (k - g + 1) * rows, :]).astype(jnp.bfloat16)
            if k == 0:
                mixed_ref[...] = mixed
            inner = rms_norm(mixed.astype(jnp.float32), gain_e_ref[...]).astype(jnp.bfloat16)
            place = k % (blocks // halves) * rows
            inner_refs[k * halves // blocks][place : place + rows, :] = inner
            prob = jax.nn.sigmoid(dot(router_ref[...], inner, 1))
            expert = lax.broadcasted_iota(jnp.int32, (LANES, rows), 0).astype(jnp.float32)
            ids = token_refs[k][rows : rows + EXTRA, :].astype(jnp.float32)
            chosen = (ids[0:1, 0:rows] == expert) | (ids[1:2, 0:rows] == expert)
            weight_ref[k * rows : (k + 1) * rows, :] = jnp.where(chosen, prob, 0.0).T


def front(bases, prompts, owner, gain_a, gain_e, router, pairs, pieces, tokens):
    rows = tokens[0].shape[0] - EXTRA
    width = tokens[0].shape[1]
    blocks = len(tokens)
    outs = [
        jax.ShapeDtypeStruct((rows, width), jnp.bfloat16),
        jax.ShapeDtypeStruct((blocks * rows, LANES), jnp.float32),
    ]
    halves = 2 if blocks % 2 == 0 else 1
    outs += [jax.ShapeDtypeStruct((blocks * rows // halves, width), jnp.bfloat16)] * halves
    arrays = [prompts, owner, gain_a, gain_e, router, *pairs, *pieces, *tokens]
    total = owner.shape[1]
    scratch = [pltpu.VMEM((n, width), jnp.bfloat16) for n in (total, total, blocks * rows)]
    mixed, weight, *inner = pl.pallas_call(
        functools.partial(front_kernel, len(pairs) // 2, len(pieces), blocks, rows),
        grid=(1,),
        out_shape=outs,
        in_specs=[pl.BlockSpec(memory_space=pltpu.SMEM)] + [whole(a) for a in arrays],
        out_specs=[whole(a) for a in outs],
        scratch_shapes=scratch,
        compiler_params=pltpu.CompilerParams(vmem_limit_bytes=VMEM),
        cost_estimate=brief(),
        name="front",
    )(bases, *arrays)
    return mixed, weight, inner


def hidden_kernel(los, sets, tiles, at_ref, *refs):
    x_refs, refs = refs[: sets * tiles], refs[sets * tiles :]
    weight_refs, refs = refs[:sets], refs[sets:]
    gate_refs, up_refs, refs = refs[:los], refs[los : 2 * los], refs[2 * los :]
    act_refs, gate, up = refs[:sets], refs[sets], refs[sets + 1]
    units = gate_refs[0].shape[0]

    @pl.when(pl.program_id(0) == 0)
    def _():
        for j in range(los):
            place = pl.ds(pl.multiple_of(lax.rem(at_ref[1] + j, los) * units, 16), units)
            gate[place, :] = gate_refs[j][...]
            up[place, :] = up_refs[j][...]

    for t in range(sets * tiles):

        def work(t=t):
            x = x_refs[t][...]
            lane = lax.broadcasted_iota(jnp.int32, (x.shape[0], LANES), 1)
            weight = weight_refs[t // tiles][...]
            scale = jnp.sum(jnp.where(lane == at_ref[0], weight, 0.0), axis=1, keepdims=True)
            gated = jax.nn.gelu(dot(x, gate[...], 1), approximate=True)
            act_refs[t // tiles][...] = (gated * dot(x, up[...], 1) * scale).astype(jnp.bfloat16)

        pl.when(pl.program_id(0) == t)(work)


def hidden(at, groups, gates, ups):
    sets, tiles, (tile, width) = len(groups), len(groups[0][0]), groups[0][0][0].shape
    los, units = len(gates), gates[0].shape[0]
    xs = [x for group, _ in groups for x in group]
    once = lambda a: pl.BlockSpec(a.shape, lambda i: (0, 0), pipeline_mode=pl.Buffered(1))
    place = lambda n: lambda i: (jnp.clip(i - n * tiles, 0, tiles - 1), 0)
    return pl.pallas_call(
        functools.partial(hidden_kernel, los, sets, tiles),
        grid=(sets * tiles,),
        out_shape=[jax.ShapeDtypeStruct((tiles * tile, los * units), jnp.bfloat16)] * sets,
        in_specs=[pl.BlockSpec(memory_space=pltpu.SMEM)]
        + [once(x) for x in xs]
        + [pl.BlockSpec((tile, LANES), place(n)) for n in range(sets)]
        + [once(a) for a in (*gates, *ups)],
        out_specs=[pl.BlockSpec((tile, los * units), place(n)) for n in range(sets)],
        scratch_shapes=[pltpu.VMEM((los * units, width), jnp.bfloat16)] * 2,
        compiler_params=pltpu.CompilerParams(vmem_limit_bytes=VMEM // 2),
        cost_estimate=brief(),
        name="hidden",
    )(at, *xs, *(w for _, w in groups), *gates, *ups)


def final_kernel(los, lines, count, lo_ref, mixed_ref, *refs):
    out_ref = refs[-1]
    cols = mixed_ref.shape[1] // (los * lines)
    for j in range(los):
        parts = refs[j * count : (j + 1) * count]
        total = parts[0][...].astype(jnp.float32)
        for part in parts[1:]:
            total = total + part[...].astype(jnp.float32)
        for h in range(lines):
            first = (h * los + lax.rem(lo_ref[0] + j, los)) * cols
            place = pl.ds(pl.multiple_of(first, LANES), cols)
            own = mixed_ref[:, place].astype(jnp.float32)
            out_ref[:, place] = (own + total[:, h * cols : (h + 1) * cols]).astype(jnp.bfloat16)


def final(lines, lo, mixed, parts):
    los, count = len(parts), len(parts[0])
    rows, width = mixed.shape
    if width // (los * lines) % LANES:
        sums = [sum(p.astype(jnp.float32) for p in group).reshape(rows, lines, -1) for group in parts]
        total = jnp.roll(jnp.stack(sums, axis=2), lo[0], axis=2).reshape(rows, width)
        return (mixed.astype(jnp.float32) + total).astype(jnp.bfloat16)
    flat = [p for group in parts for p in group]
    return pl.pallas_call(
        functools.partial(final_kernel, los, lines, count),
        out_shape=jax.ShapeDtypeStruct(mixed.shape, jnp.bfloat16),
        grid=(1,),
        in_specs=[pl.BlockSpec(memory_space=pltpu.SMEM)] + [whole(a) for a in (mixed, *flat)],
        out_specs=whole(mixed),
        compiler_params=pltpu.CompilerParams(vmem_limit_bytes=VMEM // 4),
        cost_estimate=brief(),
        name="final",
    )(lo, mixed, *flat)


def on_device(
    sizes,
    residual_input,
    prompt_token_length,
    prompt_adapter_index,
    adapter_table_row,
    adapter_norm_gain,
    adapter_down_maps,
    adapter_up_maps,
    expert_norm_gain,
    router,
    token_expert_index,
    expert_gate_up_weight,
    expert_down_weight,
):
    lines, los, exs = sizes["line"], sizes["lo"], sizes["ex"]
    tok_rows, width = residual_input.shape
    num_experts = router.shape[1]
    line, lo, ex, core = (lax.axis_index(n) for n in ("line", "lo", "ex", "core"))

    down_rows = expert_down_weight.shape[1]
    cols = expert_down_weight.shape[2]
    slots, rank, _ = adapter_down_maps.shape
    shares = los if slots % los == 0 else 1
    share = slots // shares
    ex_far, lo_far = range(1, exs), range(1, los)

    ids = token_expert_index.T.astype(jnp.bfloat16)
    ids = jnp.pad(ids, ((0, EXTRA - ids.shape[0]), (0, width - tok_rows)))
    block = jnp.concatenate([residual_input, ids])
    maps = [m.reshape(slots * rank, width) for m in (adapter_down_maps, adapter_up_maps)]
    first = lo * share * rank if shares > 1 else 0
    sent = lax.dynamic_slice_in_dim(jnp.stack(maps), first, share * rank, axis=1)
    crossed = [from_offset(sent, "ex", exs, i) for i in ex_far]
    gate, up = expert_gate_up_weight[0, 0].T, expert_gate_up_weight[0, 1].T
    ups = {(0, j): from_offset(up, "lo", los, j) for j in lo_far}
    tokens = {m: across(block, lines, m) for m in (2, 1, 0) if m < lines}
    other_maps = [from_offset(m, "core", CORES, 1) for m in maps]

    ends = jnp.cumsum(prompt_token_length)
    adapter_ids = jnp.arange(adapter_table_row.shape[0], dtype=jnp.int32)
    named = prompt_adapter_index[:, None] == adapter_ids[None, :]
    prompt_row = jnp.sum(jnp.where(named, adapter_table_row[None, :], 0), axis=1)
    prompts = jnp.stack([ends - prompt_token_length, ends, prompt_row])
    router_rows = jnp.pad(router.T, ((0, LANES - num_experts), (0, 0)))
    offsets = line ^ jnp.arange(lines, dtype=jnp.int32)
    bases = (((offsets * los + lo) * exs + ex) * CORES + core) * tok_rows
    number = jnp.arange(slots * rank, dtype=jnp.int32) // rank
    both = lambda slot: [slot, slot + jnp.where(core == 0, slots, -slots)]
    owners = both((ex * CORES + core) * slots + number)
    for i in ex_far:
        for j in range(shares):
            start = ((ex + i) % exs * CORES + core) * slots + (lo + j) % los * share
            owners += both(start + number[: share * rank])
    owner = jnp.concatenate(owners)[None, :]
    small = [bases, prompts, owner, adapter_norm_gain[None], expert_norm_gain[None], router_rows]

    passed = [from_offset(c, "lo", los, j) for c in crossed for j in range(shares)]
    gate, up, small, ups, tokens, other_maps = together(gate, up, small, ups, tokens, other_maps)
    gates = {(i, 0): from_offset(gate, "ex", exs, i) for i in ex_far}
    if lines == 4:
        tokens[3] = across(tokens[2], lines, 1)
    held = [v for p in passed for v in (p, from_offset(p, "core", CORES, 1))]

    gates, tokens, held, gate, up, down = together(gates, tokens, held, gate, up, expert_down_weight)
    gates.update({(0, j): from_offset(gate, "lo", los, j) for j in lo_far})
    ups.update({(i, 0): from_offset(up, "ex", exs, i) for i in ex_far})
    down = lax.all_to_all(
        down.reshape(lines, down_rows // lines, cols), "line", split_axis=0, concat_axis=0, tiled=True
    )
    mixed, w_own, x_own = front(*small, maps + other_maps, held, [tokens[m] for m in range(lines)])

    gates, ups, gate, up, x_own, w_own = together(gates, ups, gate, up, x_own, w_own)
    gates[0, 0], ups[0, 0] = gate, up
    for i in ex_far:
        for j in lo_far:
            gates[i, j] = from_offset(gates[i, 0], "lo", los, j)
            ups[i, j] = from_offset(ups[0, j], "ex", exs, i)
    x_far = [from_offset(v, "core", CORES, 1) for v in x_own]
    w_far = from_offset(w_own, "core", CORES, 1)

    def act(i, *groups):
        at = jnp.stack([(ex + i) % exs * CORES + core, lo])
        return hidden(at, groups, *([of[i, j] for j in range(los)] for of in (gates, ups)))

    near, far = act(0, (x_own, w_own)), act(0, (x_far, w_far))
    down = down.transpose(1, 0, 2).reshape(down_rows // lines, lines * cols)
    downs = {(i, 0): from_offset(down, "ex", exs, i) for i in range(exs)}
    downs.update({(0, j): from_offset(down, "lo", los, j) for j in lo_far})
    places = [(a, b) for a in range(los) for b in range(exs)]
    for i in ex_far:
        for j in lo_far:
            moves = [((a + j) % los * exs + (b + i) % exs, a * exs + b) for a, b in places]
            downs[i, j] = lax.ppermute(down, ("lo", "ex"), moves)

    x_own, w_own, x_far, w_far, near, far, gates, ups = together(x_own, w_own, x_far, w_far, near, far, gates, ups)
    for i in ex_far:
        later = act(i, (x_far, w_far), (x_own, w_own))
        far, near = [*far, later[0]], [*near, later[1]]

    direct = [(i, 0) for i in range(exs)] + [(0, j) for j in lo_far]
    near, far, pieces = together(near, far, [downs[k] for k in direct])
    downs.update(zip(direct, pieces))
    parts = []
    joined = None
    for j in range(los):
        of_piece = [downs[i, j] for i in range(exs)]
        if joined is not None:
            near, far, of_piece, joined = together(near, far, of_piece, joined)
            parts[-1].append(across(joined, lines, 2))
        sums = lambda acts: sum(dot(a, d) for a, d in zip(acts, of_piece))
        sent = sums(far).astype(jnp.bfloat16).reshape(lines, tok_rows, -1)
        added = jnp.concatenate([from_offset(sent[k], "core", CORES, 1) for k in range(lines)])
        total = (sums(near) + added.astype(jnp.float32)).astype(jnp.bfloat16)
        home = list(total.reshape(lines, tok_rows, -1))
        if lines == 4:
            passing = across(home[3], lines, 1)
            if j > 0:
                passing, parts[-1] = together(passing, parts[-1])
            joined = add(home[2], passing)
            parts.append([home[0], across(home[1], lines, 1)])
        else:
            parts.append([across(home[m], lines, m) for m in range(lines)])
    if lines == 4:
        parts[-1].append(across(joined, lines, 2))
    return final(lines, lo[None], mixed, parts)


def solution(mesh):
    dp, expert = mesh.shape["dp"], mesh.shape["expert"]
    lines = 4 if dp % 4 == 0 else 2 if dp % 2 == 0 else 1
    sizes = {"line": lines, "lo": dp // lines, "ex": expert // CORES, "core": CORES}
    inner = Mesh(mesh.devices.reshape(tuple(sizes.values())), tuple(sizes))
    rows = P(("line", "lo", "ex", "core"), None)
    slots = P(("ex", "core"), None, None)
    placed = (
        rows,
        P(),
        P(),
        P(),
        P(),
        slots,
        slots,
        P(),
        P(),
        rows,
        P(("ex", "core"), None, None, ("line", "lo")),
        P(("ex", "core"), None, ("line", "lo")),
    )

    def body(*arrays):
        return on_device(sizes, *arrays)

    return jax.shard_map(body, mesh=inner, in_specs=placed, out_specs=rows, check_vma=False)
```
